32 devices in a mesh: stream: 16 (over z, y, core), batch: 2 (over x).
Axes of the slice: x: 2, y: 2, z: 4, core: 2. Of those that a mesh axis runs over, the one named last changes fastest.
Arguments:
- images: bfloat16 [576, 13, 13, 512], P(('stream', 'batch')), may hold values from -6 to 6
- conv4_weight: bfloat16 [4608, 1024], P('stream'), may hold values from -0.09375 to 0.09375
- conv4_bias: bfloat16 [1024], P('stream'), may hold values from -3 to 3
- conv5_weight: bfloat16 [4608, 1024], P('stream'), may hold values from -0.09375 to 0.09375
- conv5_bias: bfloat16 [1024], P('stream'), may hold values from -3 to 3
- cotangent: bfloat16 [576, 13, 13, 512], P(('stream', 'batch')), may hold values from -6 to 6
Outputs:
- conv5_out: bfloat16 [576, 13, 13, 512], P(('stream', 'batch'))
- images_grad: bfloat16 [576, 13, 13, 512], P(('stream', 'batch'))
- conv4_weight_grad: float32 [4608, 1024], P('stream')
- conv4_bias_grad: float32 [1024], P('stream')
- conv5_weight_grad: float32 [4608, 1024], P('stream')
- conv5_bias_grad: float32 [1024], P('stream')
The draws below stay inside these ranges and needn't reach their ends.
All inputs are finite; a program needn't handle non-finite values.
Results may differ from the reference program's by a relative error of at most 0.0095.
Values may be sent and summed in bfloat16 or wider, within the bound.
A program may use at most 320 MiB of HBM per device.

```python
from functools import partial
import jax
import jax.numpy as jnp
from jax import lax

CH = 512
SIDE = 13
IMG_MB = 6
ITEMS = 576


def block_levels(own_key, dims, cuts, smallest, high):
    level, own = 1.0, jax.random.fold_in(own_key, 6)
    for dim, parts in cuts:
        draws = jnp.exp(jax.random.uniform(jax.random.fold_in(own, dim), (parts,), jnp.float32, smallest / len(cuts), high / len(cuts)))
        level = level * jnp.repeat(draws, dims[dim] // parts).reshape([-1 if axis == dim else 1 for axis in range(len(dims))])
    return level


def normal_values(key, shape, width, reach, shards=(), held_as=jnp.bfloat16):
    entries = jax.random.normal(key, shape, jnp.float32) * width
    if len(shards) > 0:
        entries = block_levels(key, shape, shards, -0.22, 0.18) * entries
    return jnp.clip(entries, min=-reach, max=reach).astype(held_as)


def setup_inputs(seed: int = 0) -> dict:
    keys = jax.random.split(jax.random.key(seed), 7)
    images = normal_values(keys[0], (ITEMS, SIDE, SIDE, CH), 1.0, 6.0, ((0, 32),))
    conv4_weight = normal_values(keys[1], (9 * CH, 2 * CH), (9 * CH) ** -0.5, 0.09375, ((0, 16),))
    conv4_bias = normal_values(keys[2], (2 * CH,), 0.5, 3.0, ((0, 16),))
    conv5_weight = normal_values(keys[3], (9 * CH, 2 * CH), (9 * CH) ** -0.5, 0.09375, ((0, 16),))
    conv5_bias = normal_values(keys[4], (2 * CH,), 0.5, 3.0, ((0, 16),))
    cotangent = normal_values(keys[5], (ITEMS, SIDE, SIDE, CH), 1.0, 6.0, ((0, 32),))
    return dict(images=images, conv4_weight=conv4_weight, conv4_bias=conv4_bias, conv5_weight=conv5_weight, conv5_bias=conv5_bias, cotangent=cotangent)


@jax.custom_vjp
def low(v):
    return lax.optimization_barrier(v.astype(jnp.bfloat16)).astype(jnp.float32)

@jax.custom_vjp
def low_back(v):
    return v

def low_keep(v):
    return (low(v), None)

def low_pass(kept, grad):
    return (grad,)

def back_keep(v):
    return (v, None)

def back_low(kept, grad):
    return (low(grad),)
low.defvjp(low_keep, low_pass)
low_back.defvjp(back_keep, back_low)

def patch_rows(field):
    image_count = field.shape[0]
    padded = jnp.pad(field, ((0, 0), (1, 1), (1, 1), (0, 0)))
    tap_list = [padded[:, row_off:row_off + SIDE, col_off:col_off + SIDE, :] for row_off in range(3) for col_off in range(3)]
    return jnp.stack(tap_list, 3).reshape(image_count * SIDE * SIDE, 9 * CH)

def conv_layer(field, weight, bias_row):
    product = jnp.dot(patch_rows(field), weight, precision=lax.Precision.HIGHEST) + bias_row
    return product.reshape(field.shape)

def block_forward(field, weight_four, bias_four, weight_five, bias_five):
    pre_four = low_back(conv_layer(field, weight_four, bias_four))
    hidden = low(jax.nn.gelu(pre_four))
    pre_five = low_back(conv_layer(hidden, weight_five, bias_five))
    return jax.nn.gelu(pre_five)

def forward(images, conv4_weight, conv4_bias, conv5_weight, conv5_bias):
    blocks = images.reshape(2, -1, IMG_MB, SIDE, SIDE, CH)
    biases_four = conv4_bias.reshape(2, CH)
    biases_five = conv5_bias.reshape(2, CH)
    results = []
    for stream_id in range(2):
        kernel_four = conv4_weight[:, stream_id * CH:(stream_id + 1) * CH]
        kernel_five = conv5_weight[:, stream_id * CH:(stream_id + 1) * CH]
        block_fn = jax.checkpoint(partial(block_forward, weight_four=kernel_four, bias_four=biases_four[stream_id], weight_five=kernel_five, bias_five=biases_five[stream_id]))
        results.append(lax.map(block_fn, blocks[stream_id]))
    return jnp.stack(results).reshape(images.shape)

def reference(images, conv4_weight, conv4_bias, conv5_weight, conv5_bias, cotangent):
    result, pullback = jax.vjp(forward, images.astype(jnp.float32), conv4_weight.astype(jnp.float32), conv4_bias.astype(jnp.float32), conv5_weight.astype(jnp.float32), conv5_bias.astype(jnp.float32))
    grads = pullback(cotangent.astype(jnp.float32))
    return (result.astype(jnp.bfloat16), grads[0].astype(jnp.bfloat16), grads[1], grads[2], grads[3], grads[4])
```

```python
import functools
import jax
import jax.numpy as jnp
import numpy as np
from jax import lax
from jax.experimental import pallas as pl
from jax.experimental.pallas import tpu as pltpu
from jax.sharding import PartitionSpec as P

CH = 512
SIDE = 13
ROOT = 0.7978845608
CUBE = 0.044715
f32 = jnp.float32
bf16 = jnp.bfloat16


def tanh_part(v, v2):
    return jnp.tanh(v * (ROOT + (ROOT * CUBE) * v2))


def gelu(v):
    half = 0.5 * v
    return half + half * tanh_part(v, v * v)


def gelu_both(v):
    v2 = v * v
    t = tanh_part(v, v2)
    half = 0.5 * v
    value = half + half * t
    slope = 0.5 + 0.5 * t + half * (1.0 - t * t) * (ROOT + (3 * ROOT * CUBE) * v2)
    return value, slope


def gelu_slope(v):
    return gelu_both(v)[1]


class Sizes:
    def __init__(self, clips):
        self.clips = clips
        self.used = clips * SIDE
        self.rows = -(-self.used // 16) * 16
        self.lanes = -(-self.rows // 256) * 256


def mask_rows(sz):
    row = np.arange(sz.rows)
    col = row % SIDE
    keep = row < sz.used
    table = np.stack([keep & (col != 0), keep, keep & (col != SIDE - 1)])
    return jnp.asarray(np.broadcast_to(table[:, :, None], (3, sz.rows, 128)), f32)


def spread(sz, dst, block, value, mask):
    rows = sz.rows
    where = pl.ds(pl.multiple_of(block * rows, 16), rows)
    for part in range(CH // 128):
        lane = part * 128
        x = value[:, lane : lane + 128]
        dst[where, lane : lane + 128] = (pltpu.roll(x, 1, 0) * mask[0]).astype(bf16)
        dst[where, CH + lane : CH + lane + 128] = (x * mask[1]).astype(bf16)
        dst[where, 2 * CH + lane : 2 * CH + lane + 128] = (
            pltpu.roll(x, rows - 1, 0) * mask[2]
        ).astype(bf16)


def turn(sz, dst, row, value, mask):
    kept = jnp.concatenate([value[:, k : k + 128] * mask[1] for k in range(0, CH, 128)], 1)
    full = jnp.concatenate([kept, jnp.zeros((sz.lanes - sz.rows, CH), f32)], 0).astype(bf16)
    dst[:, pl.ds(pl.multiple_of(row * sz.lanes, 128), sz.lanes)] = full.T


def flatten(sz, flat, stage):
    for n in range(sz.clips):
        flat[n * SIDE : (n + 1) * SIDE, :] = stage[n].astype(f32)


def unflatten(sz, stage, flat):
    for n in range(sz.clips):
        stage[n] = flat[n * SIDE : (n + 1) * SIDE, :].astype(bf16)


def fold8(value):
    return jnp.sum(value.reshape(value.shape[0] // 8, 8, CH), axis=0)


def rows13(product, finish, accs):
    accs[0][...] = product(0, skip=0)

    def pair(t, carry):
        i = 2 * t
        accs[1][...] = product(i + 1)
        finish(i, accs[0], 0)
        accs[0][...] = product(i + 2)
        finish(i + 1, accs[1], 1)
        return carry

    lax.fori_loop(0, 5, pair, 0)
    accs[1][...] = product(11)
    finish(10, accs[0], 0)
    accs[0][...] = product(12, skip=2)
    finish(11, accs[1], 1)
    finish(12, accs[0], 0)


def kernel(
    sz,
    images, cot, w4, w5, b4, b5, masks,
    out, igrad, dw4, dw5, db4, db5,
    pbuf, qbuf, xt, ht, pre4, acc0, acc1, flat_in, flat_out, stage_in, stage_out, in_sem, out_sem,
):
    rows, lanes = sz.rows, sz.lanes
    accs = (acc0, acc1)
    flats = (flat_in.at[0], flat_in.at[1])
    zero = jnp.zeros((rows, 3 * CH), bf16)
    for buf in (pbuf, qbuf):
        buf[0:rows, :] = zero
        buf[14 * rows : 15 * rows, :] = zero
        buf[15 * rows : 15 * rows + lanes - rows, :] = zero[: lanes - rows]
    flat_in[...] = jnp.zeros_like(flat_in)

    def fetch(src, i, slot):
        return pltpu.make_async_copy(src.at[:, i], stage_in.at[slot], in_sem.at[slot])

    def put(dst, i, slot):
        return pltpu.make_async_copy(stage_out.at[slot], dst.at[:, i], out_sem.at[slot])

    fetch(images, 0, 0).start()
    fetch(images, 1, 1).start()

    def prepare(i, slot):
        fetch(images, i, slot).wait()
        flatten(sz, flat_in.at[slot], stage_in.at[slot])
        fetch(images, jnp.minimum(i + 2, 12), slot).start()
        value = flat_in[slot]
        spread(sz, pbuf, i + 1, value, masks)
        turn(sz, xt, i, value, masks)

    def prepare_pair(t, carry):
        prepare(2 * t, 0)
        prepare(2 * t + 1, 1)
        return carry

    lax.fori_loop(0, 6, prepare_pair, 0)
    prepare(12, 0)
    fetch(images, 12, 1).wait()
    fetch(images, 12, 0).wait()

    fetch(cot, 0, 0).start()
    fetch(cot, 1, 1).start()

    def conv(src, w):
        def product(i, skip=None):
            total = None
            for a in range(3):
                if a == skip:
                    continue
                at = (i + a) * rows
                at = pl.multiple_of(at, 16)
                term = jnp.dot(
                    src[pl.ds(at, rows), :],
                    w[a * 3 * CH : (a + 1) * 3 * CH, :],
                    preferred_element_type=f32,
                )
                total = term if total is None else total + term
            return total

        return product

    def back(src, w):
        def product(i, skip=None):
            total = None
            for a in range(3):
                if skip is not None and a == 2 - skip:
                    continue
                at = pl.multiple_of((i + 2 - a) * rows, 16)
                for b in range(3):
                    tap = 3 * a + b
                    term = lax.dot_general(
                        src[pl.ds(at, rows), (2 - b) * CH : (3 - b) * CH],
                        w[tap * CH : (tap + 1) * CH, :],
                        (((1,), (1,)), ((), ())),
                        preferred_element_type=f32,
                    )
                    total = term if total is None else total + term
            return total

        return product

    def wgrad(left, src, dst):
        for a in range(3):

            def one(b, carry):
                total = None
                for q in range(13):
                    block = q + 2 - a
                    if block == 0 or block == 14:
                        continue
                    term = jnp.dot(
                        left[:, q * lanes : (q + 1) * lanes],
                        src[block * rows : block * rows + lanes,
                            pl.ds(pl.multiple_of((2 - b) * CH, CH), CH)],
                        preferred_element_type=f32,
                    )
                    total = term if total is None else total + term
                at = pl.multiple_of((3 * a + b) * CH, CH)
                dst[pl.ds(at, CH), :] = total.astype(dst.dtype)
                return carry

            lax.fori_loop(0, 3, one, 0)

    def finish4(i, acc, slot):
        v = acc[...] + b4[...]
        pre4[pl.ds(pl.multiple_of(i * rows, 16), rows), :] = v
        h = gelu(v)
        spread(sz, qbuf, i + 1, h, masks)
        turn(sz, ht, i, h, masks)

    rows13(conv(pbuf, w4), finish4, accs)

    put(out, 0, 0).start()
    put(out, 1, 1).start()
    db5[...] = jnp.zeros_like(db5)

    def finish5(i, acc, slot):
        put(out, i, slot).wait()
        fetch(cot, i, slot).wait()
        flatten(sz, flat_in.at[slot], stage_in.at[slot])
        fetch(cot, jnp.minimum(i + 2, 12), slot).start()
        value, slope = gelu_both(acc[...] + b5[...])
        flat_out[slot] = value
        unflatten(sz, stage_out.at[slot], flat_out.at[slot])
        put(out, i, slot).start()
        g = flat_in[slot] * slope
        g = g.astype(bf16).astype(f32)
        db5[...] += fold8(g)
        spread(sz, pbuf, i + 1, g, masks)

    rows13(conv(qbuf, w5), finish5, accs)
    fetch(cot, 12, 1).wait()
    fetch(cot, 12, 0).wait()

    wgrad(ht, pbuf, dw5)
    db4[...] = jnp.zeros_like(db4)

    def finish_back5(i, acc, slot):
        g = acc[...] * gelu_slope(pre4[pl.ds(pl.multiple_of(i * rows, 16), rows), :])
        g = jnp.concatenate([g[:, k : k + 128] * masks[1] for k in range(0, CH, 128)], 1)
        g = g.astype(bf16).astype(f32)
        db4[...] += fold8(g)
        spread(sz, qbuf, i + 1, g, masks)

    rows13(back(pbuf, w5), finish_back5, accs)
    wgrad(xt, qbuf, dw4)

    put(out, 12, 1).wait()
    put(out, 12, 0).wait()
    put(igrad, 0, 0).start()
    put(igrad, 1, 1).start()

    def finish_back4(i, acc, slot):
        put(igrad, i, slot).wait()
        flat_out[slot] = acc[...]
        unflatten(sz, stage_out.at[slot], flat_out.at[slot])
        put(igrad, i, slot).start()

    rows13(back(qbuf, w4), finish_back4, accs)
    put(igrad, 12, 1).wait()
    put(igrad, 12, 0).wait()


def block(images, cot, w4, w5, b4, b5):
    sz = Sizes(images.shape[0])
    rows, lanes = sz.rows, sz.lanes
    vm = pl.BlockSpec(memory_space=pltpu.VMEM)
    hb = pl.BlockSpec(memory_space=pl.ANY)
    return pl.pallas_call(
        functools.partial(kernel, sz),
        out_shape=(
            jax.ShapeDtypeStruct(images.shape, bf16),
            jax.ShapeDtypeStruct(images.shape, bf16),
            jax.ShapeDtypeStruct((9 * CH, CH), bf16),
            jax.ShapeDtypeStruct((9 * CH, CH), bf16),
            jax.ShapeDtypeStruct((8, CH), f32),
            jax.ShapeDtypeStruct((8, CH), f32),
        ),
        in_specs=[hb, hb, vm, vm, vm, vm, vm],
        out_specs=(hb, hb, vm, vm, vm, vm),
        scratch_shapes=[
            pltpu.VMEM((15 * rows + lanes - rows, 3 * CH), bf16),
            pltpu.VMEM((15 * rows + lanes - rows, 3 * CH), bf16),
            pltpu.VMEM((CH, SIDE * lanes), bf16),
            pltpu.VMEM((CH, SIDE * lanes), bf16),
            pltpu.VMEM((SIDE * rows, CH), f32),
            pltpu.VMEM((rows, CH), f32),
            pltpu.VMEM((rows, CH), f32),
            pltpu.VMEM((2, rows, CH), f32),
            pltpu.VMEM((2, rows, CH), f32),
            pltpu.VMEM((2, sz.clips, SIDE, CH), bf16),
            pltpu.VMEM((2, sz.clips, SIDE, CH), bf16),
            pltpu.SemaphoreType.DMA((2,)),
            pltpu.SemaphoreType.DMA((2,)),
        ],
        compiler_params=pltpu.CompilerParams(vmem_limit_bytes=63 << 20),
    )(images, cot, w4, w5, b4.reshape(1, CH).astype(f32), b5.reshape(1, CH).astype(f32), mask_rows(sz))


def shards(images, conv4_weight, conv4_bias, conv5_weight, conv5_bias, cotangent):
    half = lax.axis_size("stream") // 2
    group = lax.axis_index("stream") // half
    weights = lax.all_gather(
        jnp.concatenate([conv4_weight, conv5_weight], 1), "stream", axis=0, tiled=True
    )
    biases = lax.all_gather(jnp.stack([conv4_bias, conv5_bias], 1), "stream", axis=0, tiled=True)
    w4 = lax.dynamic_slice_in_dim(weights, group * CH, CH, 1)
    w5 = lax.dynamic_slice_in_dim(weights, (group + 2) * CH, CH, 1)
    own = lax.dynamic_slice_in_dim(biases, group * CH, CH, 0)
    out, igrad, dw4, dw5, db4, db5 = block(images, cotangent, w4, w5, own[:, 0], own[:, 1])

    def widen(value):
        value = value.astype(f32)
        blank = jnp.zeros_like(value)
        return jnp.where(
            group == 0,
            jnp.concatenate([value, blank], -1),
            jnp.concatenate([blank, value], -1),
        )

    def reduce(value):
        value = lax.psum_scatter(widen(value), "stream", scatter_dimension=0, tiled=True)
        return lax.psum(value.astype(bf16), "batch").astype(f32)

    dw4, dw5 = reduce(dw4), reduce(dw5)
    db = lax.psum(jnp.stack([widen(db4.sum(0)), widen(db5.sum(0))]), ("stream", "batch"))
    size = conv4_bias.shape[0]
    db = lax.dynamic_slice_in_dim(db, lax.axis_index("stream") * size, size, 1)
    return out, igrad, dw4, db[0], dw5, db[1]


def solution(mesh):
    clip = P(("stream", "batch"), None, None, None)
    weight = P("stream", None)
    bias = P("stream")
    return jax.shard_map(
        shards,
        mesh=mesh,
        in_specs=(clip, weight, bias, weight, bias, clip),
        out_specs=(clip, clip, weight, bias, weight, bias),
        check_vma=False,
    )
```

```python
import functools
import jax
import jax.numpy as jnp
import numpy as np
from jax import lax
from jax.experimental import pallas as pl
from jax.experimental.pallas import tpu as pltpu
from jax.sharding import PartitionSpec as P

CH = 512
SIDE = 13
TAPS = 9
ROOT = 0.7978845608
CUBE = 0.044715
VMEM_LIMIT = 64 << 20
f32 = jnp.float32
bf16 = jnp.bfloat16
MESH = pl.DeviceIdType.MESH


def tanh_part(v, v2):
    return jnp.tanh(v * (ROOT + (ROOT * CUBE) * v2))


def gelu(v):
    half = 0.5 * v
    return half + half * tanh_part(v, v * v)


def gelu_both(v):
    v2 = v * v
    t = tanh_part(v, v2)
    half = 0.5 * v
    value = half + half * t
    slope = 0.5 + 0.5 * t + half * (1.0 - t * t) * (ROOT + (3 * ROOT * CUBE) * v2)
    return value, slope


class Sizes:
    def __init__(self, clips):
        self.clips = clips
        self.used = clips * SIDE
        self.rows = -(-self.used // 16) * 16
        self.lanes = -(-self.rows // 256) * 256
        self.tall = 15 * self.rows + self.lanes - self.rows


def mask_rows(sz):
    row = np.arange(sz.rows)
    col = row % SIDE
    keep = row < sz.used
    table = np.stack([keep & (col != 0), keep, keep & (col != SIDE - 1)])
    return jnp.asarray(np.broadcast_to(table[:, :, None], (3, sz.rows, 128)), f32)


def aligned(index, size):
    return pl.ds(pl.multiple_of(index * size, size), size)


def flatten(sz, flat, stage):
    for n in range(sz.clips):
        flat[n * SIDE : (n + 1) * SIDE, :] = stage[n].astype(f32)


def unflatten(sz, stage, flat):
    for n in range(sz.clips):
        stage[n] = flat[n * SIDE : (n + 1) * SIDE, :].astype(bf16)


def fold8(value):
    return jnp.sum(value.reshape(value.shape[0] // 8, 8, CH), axis=0)


def nothing(step):
    return None


class Work:
    def __init__(self, sz, images, cot, masks, out, igrad, bufs):
        self.sz = sz
        self.images, self.cot, self.out, self.igrad = images, cot, out, igrad
        self.masks = masks
        (self.pbuf, self.qbuf, self.xt, self.ht, self.pre4, acc0, acc1, self.flat_in,
         self.stage_in, self.stage_out, self.in_sem, self.out_sem) = bufs
        self.accs = (acc0, acc1)

    @staticmethod
    def buffers(sz):
        rows, lanes = sz.rows, sz.lanes
        return [
            pltpu.VMEM((sz.tall, 3 * CH), bf16),
            pltpu.VMEM((sz.tall, 3 * CH), bf16),
            pltpu.VMEM((CH, SIDE * lanes), bf16),
            pltpu.VMEM((CH, SIDE * lanes), bf16),
            pltpu.VMEM((SIDE * rows, CH), f32),
            pltpu.VMEM((rows, CH), f32),
            pltpu.VMEM((rows, CH), f32),
            pltpu.VMEM((2, rows, CH), f32),
            pltpu.VMEM((2, sz.clips, SIDE, CH), bf16),
            pltpu.VMEM((2, sz.clips, SIDE, CH), bf16),
            pltpu.SemaphoreType.DMA((2,)),
            pltpu.SemaphoreType.DMA((2,)),
        ]

    def clear(self):
        sz, rows = self.sz, self.sz.rows
        for buf in (self.pbuf, self.qbuf):
            buf[0:rows, :] = jnp.zeros((rows, 3 * CH), bf16)
            buf[14 * rows : sz.tall, :] = jnp.zeros((sz.tall - 14 * rows, 3 * CH), bf16)
        self.flat_in[...] = jnp.zeros_like(self.flat_in)

    def fetch(self, src, i, slot):
        return pltpu.make_async_copy(src.at[:, i], self.stage_in.at[slot], self.in_sem.at[slot])

    def put(self, dst, i, slot):
        return pltpu.make_async_copy(self.stage_out.at[slot], dst.at[:, i], self.out_sem.at[slot])

    def fetch_two(self, src):
        self.fetch(src, 0, 0).start()
        self.fetch(src, 1, 1).start()

    def fetch_end(self, src):
        self.fetch(src, 12, 1).wait()
        self.fetch(src, 12, 0).wait()

    def put_two(self, dst):
        self.put(dst, 0, 0).start()
        self.put(dst, 1, 1).start()

    def put_end(self, dst):
        self.put(dst, 12, 1).wait()
        self.put(dst, 12, 0).wait()

    def spread(self, dst, block, value):
        where = aligned(block, self.sz.rows)
        for lane in range(0, CH, 128):
            x = value[:, lane : lane + 128]
            left = pltpu.roll(x, 1, 0) * self.masks[0]
            right = pltpu.roll(x, self.sz.rows - 1, 0) * self.masks[2]
            dst[where, lane : lane + 128] = left.astype(bf16)
            dst[where, CH + lane : CH + lane + 128] = (x * self.masks[1]).astype(bf16)
            dst[where, 2 * CH + lane : 2 * CH + lane + 128] = right.astype(bf16)

    def kept(self, value):
        return jnp.concatenate([value[:, k : k + 128] * self.masks[1] for k in range(0, CH, 128)], 1)

    def turn(self, dst, i, value):
        sz = self.sz
        blank = jnp.zeros((sz.lanes - sz.rows, CH), f32)
        full = jnp.concatenate([self.kept(value), blank], 0).astype(bf16)
        dst[:, aligned(i, sz.lanes)] = full.T

    def prepare(self, i, slot):
        self.fetch(self.images, i, slot).wait()
        flatten(self.sz, self.flat_in.at[slot], self.stage_in.at[slot])
        self.fetch(self.images, jnp.minimum(i + 2, 12), slot).start()
        value = self.flat_in[slot]
        self.spread(self.pbuf, i + 1, value)
        self.turn(self.xt, i, value)

    def prepare_pairs(self, first, last):
        def pair(t, carry):
            self.prepare(2 * t, 0)
            self.prepare(2 * t + 1, 1)
            return carry

        lax.fori_loop(first, last, pair, 0)

    def rows13(self, product, finish, service=nothing):
        accs = self.accs
        accs[0][...] = product(0, 0)

        def pair(t, carry):
            i = 2 * t
            service(t)
            accs[1][...] = product(i + 1)
            finish(i, accs[0], 0)
            accs[0][...] = product(i + 2)
            finish(i + 1, accs[1], 1)
            return carry

        lax.fori_loop(0, 5, pair, 0)
        service(5)
        accs[1][...] = product(11)
        finish(10, accs[0], 0)
        service(6)
        accs[0][...] = product(12, 2)
        finish(11, accs[1], 1)
        finish(12, accs[0], 0)

    def partial_rows(self, product, store, service):
        def pair(t, carry):
            service(t)
            store(2 * t, product(2 * t))
            store(2 * t + 1, product(2 * t + 1))
            return carry

        lax.fori_loop(0, 6, pair, 0)
        store(12, product(12))

    def conv(self, src, w):
        rows = self.sz.rows

        def product(i, skip=None):
            total = None
            for a in range(3):
                if a == skip:
                    continue
                term = jnp.dot(
                    src[aligned(i + a, rows), :],
                    w[a * 3 * CH : (a + 1) * 3 * CH, :],
                    preferred_element_type=f32,
                )
                total = term if total is None else total + term
            return total

        return product

    def conv_taps(self, src, w, first, count):
        rows = self.sz.rows

        def product(i, skip=None):
            total = None
            for n in range(count):
                tap = first + n
                term = jnp.dot(
                    src[aligned(i + tap // 3, rows), aligned(tap % 3, CH)],
                    w[aligned(tap, CH), :],
                    preferred_element_type=f32,
                )
                total = term if total is None else total + term
            return total

        return product

    def back(self, src, w):
        rows = self.sz.rows

        def product(i, skip=None):
            total = None
            for a in range(3):
                if skip is not None and a == 2 - skip:
                    continue
                for b in range(3):
                    tap = 3 * a + b
                    term = lax.dot_general(
                        src[aligned(i + 2 - a, rows), (2 - b) * CH : (3 - b) * CH],
                        w[tap * CH : (tap + 1) * CH, :],
                        (((1,), (1,)), ((), ())),
                        preferred_element_type=f32,
                    )
                    total = term if total is None else total + term
            return total

        return product

    def wgrad(self, left, src, dst, service=nothing):
        rows, lanes = self.sz.rows, self.sz.lanes
        for a in range(3):

            def one(b, carry, a=a):
                total = None
                for q in range(13):
                    block = q + 2 - a
                    if block == 0 or block == 14:
                        continue
                    term = jnp.dot(
                        left[:, q * lanes : (q + 1) * lanes],
                        src[block * rows : block * rows + lanes, aligned(2 - b, CH)],
                        preferred_element_type=f32,
                    )
                    total = term if total is None else total + term
                dst[aligned(3 * a + b, CH), :] = total.astype(dst.dtype)
                service(3 * a + b)
                return carry

            lax.fori_loop(0, 3, one, 0)

    def finish4(self, b4):
        def finish(i, acc, slot):
            v = acc[...] + b4
            self.pre4[aligned(i, self.sz.rows), :] = v
            h = gelu(v)
            self.spread(self.qbuf, i + 1, h)
            self.turn(self.ht, i, h)

        return finish

    def finish5(self, b5, db5):
        def finish(i, acc, slot):
            self.put(self.out, i, slot).wait()
            self.fetch(self.cot, i, slot).wait()
            flatten(self.sz, self.flat_in.at[slot], self.stage_in.at[slot])
            self.fetch(self.cot, jnp.minimum(i + 2, 12), slot).start()
            value, slope = gelu_both(acc[...] + b5)
            acc[...] = value
            unflatten(self.sz, self.stage_out.at[slot], acc)
            self.put(self.out, i, slot).start()
            g = (self.flat_in[slot] * slope).astype(bf16).astype(f32)
            db5[...] += fold8(g)
            self.spread(self.pbuf, i + 1, g)

        return finish

    def finish_back5(self, db4):
        def finish(i, acc, slot):
            g = acc[...] * gelu_both(self.pre4[aligned(i, self.sz.rows), :])[1]
            g = self.kept(g).astype(bf16).astype(f32)
            db4[...] += fold8(g)
            self.spread(self.qbuf, i + 1, g)

        return finish

    def finish_back4(self, i, acc, slot):
        self.put(self.igrad, i, slot).wait()
        unflatten(self.sz, self.stage_out.at[slot], acc)
        self.put(self.igrad, i, slot).start()


def alone_kernel(sz, images, cot, w4, w5, b4, b5, masks, out, igrad, dw4, dw5, db4, db5, *bufs):
    work = Work(sz, images, cot, masks, out, igrad, bufs)
    work.clear()
    work.fetch_two(images)
    work.prepare_pairs(0, 6)
    work.prepare(12, 0)
    work.fetch_end(images)
    work.fetch_two(cot)
    work.rows13(work.conv(work.pbuf, w4), work.finish4(b4[...]))
    work.put_two(out)
    db5[...] = jnp.zeros_like(db5)
    work.rows13(work.conv(work.qbuf, w5), work.finish5(b5[...], db5))
    work.fetch_end(cot)
    work.wgrad(work.ht, work.pbuf, dw5)
    db4[...] = jnp.zeros_like(db4)
    work.rows13(work.back(work.pbuf, w5), work.finish_back5(db4))
    work.wgrad(work.xt, work.qbuf, dw4)
    work.put_end(out)
    work.put_two(igrad)
    work.rows13(work.back(work.qbuf, w4), work.finish_back4)
    work.put_end(igrad)


def block(images, cot, w4, w5, b4, b5):
    sz = Sizes(images.shape[0])
    vm = pl.BlockSpec(memory_space=pltpu.VMEM)
    hb = pl.BlockSpec(memory_space=pl.ANY)
    return pl.pallas_call(
        functools.partial(alone_kernel, sz),
        out_shape=(
            jax.ShapeDtypeStruct(images.shape, bf16),
            jax.ShapeDtypeStruct(images.shape, bf16),
            jax.ShapeDtypeStruct((TAPS * CH, CH), bf16),
            jax.ShapeDtypeStruct((TAPS * CH, CH), bf16),
            jax.ShapeDtypeStruct((8, CH), f32),
            jax.ShapeDtypeStruct((8, CH), f32),
        ),
        in_specs=[hb, hb, vm, vm, vm, vm, vm],
        out_specs=(hb, hb, vm, vm, vm, vm),
        scratch_shapes=Work.buffers(sz),
        compiler_params=pltpu.CompilerParams(vmem_limit_bytes=VMEM_LIMIT),
    )(images, cot, w4, w5, b4.reshape(1, CH).astype(f32), b5.reshape(1, CH).astype(f32), mask_rows(sz))


def plain_shards(images, conv4_weight, conv4_bias, conv5_weight, conv5_bias, cotangent):
    half = lax.axis_size("stream") // 2
    group = lax.axis_index("stream") // half
    weights = lax.all_gather(
        jnp.concatenate([conv4_weight, conv5_weight], 1), "stream", axis=0, tiled=True
    )
    biases = lax.all_gather(jnp.stack([conv4_bias, conv5_bias], 1), "stream", axis=0, tiled=True)
    w4 = lax.dynamic_slice_in_dim(weights, group * CH, CH, 1)
    w5 = lax.dynamic_slice_in_dim(weights, (group + 2) * CH, CH, 1)
    own = lax.dynamic_slice_in_dim(biases, group * CH, CH, 0)
    out, igrad, dw4, dw5, db4, db5 = block(images, cotangent, w4, w5, own[:, 0], own[:, 1])

    def widen(value):
        value = value.astype(f32)
        blank = jnp.zeros_like(value)
        return jnp.where(
            group == 0,
            jnp.concatenate([value, blank], -1),
            jnp.concatenate([blank, value], -1),
        )

    def reduce(value):
        value = lax.psum_scatter(widen(value), "stream", scatter_dimension=0, tiled=True)
        return lax.psum(value.astype(bf16), "batch").astype(f32)

    dw4, dw5 = reduce(dw4), reduce(dw5)
    db = lax.psum(jnp.stack([widen(db4.sum(0)), widen(db5.sum(0))]), ("stream", "batch"))
    size = conv4_bias.shape[0]
    db = lax.dynamic_slice_in_dim(db, lax.axis_index("stream") * size, size, 1)
    return out, igrad, dw4, db[0], dw5, db[1]


class Place:
    def __init__(self):
        s = lax.axis_index("stream")
        self.x = lax.axis_index("batch")
        self.c = s % 2
        self.y = (s // 2) % 2
        self.z = s // 4
        self.low = self.z % 2
        self.group = self.z // 2
        self.z1 = self.z + 1 - 2 * self.low
        self.z2 = (self.z + 2) % 4
        self.z12 = (self.z1 + 2) % 4
        self.number = self.x * 4 + self.y * 2 + self.low
        self.lead = self.c == self.x

    def device(self, x=None, y=None, z=None, c=None):
        x = self.x if x is None else x
        y = self.y if y is None else y
        z = self.z if z is None else z
        c = self.c if c is None else c
        return {"stream": (z * 2 + y) * 2 + c, "batch": x}

    def shard(self, k, c):
        z = (self.z, self.z1, self.z, self.z1, self.z2, self.z12, self.z2, self.z12)[k]
        y = self.y if k in (0, 1, 4, 5) else 1 - self.y
        return (z * 2 + y) * 2 + c

    def cube(self, m):
        return self.device(x=m // 4, y=(m // 2) % 2, z=self.group * 2 + m % 2)


def remote(src, dst, send, recv, device):
    return pltpu.make_async_remote_copy(
        src_ref=src, dst_ref=dst, send_sem=send, recv_sem=recv, device_id=device, device_id_type=MESH
    )


class Gather:
    SENDS = 29

    def __init__(self, at, given, full, sem_local, sends, recvs, cores):
        self.at, self.given, self.full = at, given, full
        self.sem_local, self.sends, self.recvs, self.cores = sem_local, sends, recvs, cores
        self.size = given.shape[0]
        self.cut = self.size // 3 // 16 * 16

    def rows(self, shard, part):
        start = (0, self.cut, 0)[part]
        size = (self.cut, self.size - self.cut, self.size)[part]
        return pl.ds(pl.multiple_of(shard * self.size + start, 16), size)

    def mine(self, part, group):
        start = (0, self.cut, 0)[part]
        size = (self.cut, self.size - self.cut, self.size)[part]
        return self.given.at[pl.ds(start, size), aligned(group, CH)]

    def ring(self, k):
        at = self.at
        zig, way = at.device(z=at.z1), at.device(y=1 - at.y)
        return {
            0: [(1, zig, 2), (2, way, 6)],
            1: [(3, way, 8)],
            4: [(5, zig, 4), (6, way, 10)],
            5: [(7, way, 12)],
        }.get(k, [])

    def copies(self, k, part):
        at = self.at
        spot = self.full.at[self.rows(at.shard(k, at.c), part), :]
        src = self.mine(part, at.group) if k == 0 else spot
        made = [
            remote(src, spot, self.sends.at[slot + part], self.recvs.at[there, part], device)
            for there, device, slot in self.ring(k)
        ]
        if k == 0:
            made.append(
                remote(
                    self.mine(part, 1 - at.group), spot,
                    self.sends.at[part], self.recvs.at[4, part], at.device(z=at.z2),
                )
            )
        if k > 0 and part == 1:
            made.append(
                remote(spot, spot, self.sends.at[13 + k], self.recvs.at[k, 1], at.device(x=1 - at.x))
            )
        return made

    def core(self, k):
        at = self.at
        spot = self.full.at[self.rows(at.shard(k, at.c), 2), :]
        src = self.mine(2, at.group) if k == 0 else spot
        return remote(src, spot, self.sends.at[21 + k], self.cores.at[k], at.device(c=1 - at.c))

    def local(self):
        at = self.at
        spot = self.full.at[self.rows(at.shard(0, at.c), 2), :]
        return pltpu.make_async_copy(self.mine(2, at.group), spot, self.sem_local)

    def begin(self):
        for copy in self.copies(0, 0):
            copy.start()

        @pl.when(self.at.lead)
        def _():
            for copy in self.copies(0, 1):
                copy.start()

        self.core(0).start()
        self.local().start()

    def arrived(self, k, part):
        at = self.at
        spot = self.full.at[self.rows(at.shard(k, at.c), part), :]
        return remote(spot, spot, self.sends.at[0], self.recvs.at[k, part], at.device(c=1 - at.c))

    def part_a(self, k):
        self.arrived(k, 0).wait_recv()
        for copy in self.copies(k, 0):
            copy.start()

    def part_b(self, k):
        self.arrived(k, 1).wait_recv()

        @pl.when(self.at.lead)
        def _():
            for copy in self.copies(k, 1):
                copy.start()

        self.core(k).start()

    def from_core(self, k):
        at = self.at
        spot = self.full.at[self.rows(at.shard(k, 1 - at.c), 2), :]
        remote(spot, spot, self.sends.at[0], self.cores.at[k], at.device(c=1 - at.c)).wait_recv()

    def near(self):
        self.local().wait()
        for k in range(4):
            self.from_core(k)

    def far(self):
        for k in range(4, 8):
            self.from_core(k)

    def sent(self):
        for k in range(8):
            for copy in self.copies(k, 0):
                copy.wait_send()
            self.core(k).wait_send()

        @pl.when(self.at.lead)
        def _():
            for k in range(8):
                for copy in self.copies(k, 1):
                    copy.wait_send()


class Scatter:
    def __init__(self, at, part, ebuf, fbuf, total, result, cross, sems):
        self.at, self.part, self.ebuf, self.fbuf, self.total, self.result = at, part, ebuf, fbuf, total, result
        self.cross = cross
        self.core_send, self.core_recv, self.far_send, self.far_recv, self.end_send, self.end_recv = sems
        self.size = ebuf.shape[1]
        self.half = self.size // 2

    def shard(self, j, c):
        return self.part.at[pl.ds(pl.multiple_of((2 * j + c) * self.size, 16), self.size), :]

    def core(self, j):
        at = self.at
        return remote(
            self.shard(j, 1 - at.c), self.ebuf.at[j], self.core_send.at[j], self.core_recv.at[j],
            at.device(c=1 - at.c),
        )

    def give(self, j):
        self.core(j).start()

    def out(self, j, h):
        at = self.at
        z, y = j // 2, j % 2
        to_z = at.group * 2 + z % 2
        kind = (z // 2 + at.group) % 2
        start = pl.multiple_of((2 * j + at.c) * self.size + h * self.half, 16)
        copy = remote(
            self.part.at[pl.ds(start, self.half), :], self.fbuf.at[kind, at.number],
            self.far_send.at[j, h], self.far_recv.at[kind, at.number],
            at.device(x=h, y=y, z=to_z),
        )
        away = (at.x + 2 * at.y + 4 * at.z) != (h + 2 * y + 4 * to_z)
        return copy, away

    def take(self, j):
        at = self.at
        self.core(j).wait_recv()
        start = pl.multiple_of((2 * j + at.c) * self.size, 16)
        where = pl.ds(start, self.size)
        self.part[where, :] = (self.part[where, :].astype(f32) + self.ebuf[j].astype(f32)).astype(bf16)
        for h in range(2):
            copy, away = self.out(j, h)
            pl.when(away)(copy.start)

    def tap(self, t):
        @pl.when(t >= 1)
        def _():
            self.give(t - 1)

        @pl.when(t >= 2)
        def _():
            self.take(t - 2)

    def sum_far(self):
        at = self.at
        for kind in range(2):
            z = at.z if kind == 0 else at.z2
            start = pl.multiple_of(((z * 2 + at.y) * 2 + at.c) * self.size + at.x * self.half, 16)
            self.total[kind] = self.part[pl.ds(start, self.half), :].astype(f32)

        def add(m, carry):
            @pl.when(m != at.number)
            def _():
                for kind in range(2):
                    spot = self.fbuf.at[kind, m]
                    remote(
                        spot, spot, self.far_send.at[0, 0], self.far_recv.at[kind, m], at.device(c=1 - at.c)
                    ).wait_recv()
                    self.total[kind] += spot[...].astype(f32)

            return carry

        lax.fori_loop(0, 8, add, 0)
        for kind in range(2):
            self.result[kind] = self.total[kind].astype(bf16)
        self.near_x().start()
        self.across().start()

    def near_x(self):
        at = self.at
        return remote(
            self.result.at[0], self.result.at[2], self.end_send.at[0], self.end_recv.at[0], at.device(x=1 - at.x)
        )

    def across(self):
        at = self.at
        return remote(
            self.result.at[1], self.cross, self.end_send.at[1], self.end_recv.at[1], at.device(z=at.z2)
        )

    def far_x(self):
        at = self.at
        return remote(
            self.cross, self.result.at[3], self.end_send.at[2], self.end_recv.at[2], at.device(x=1 - at.x)
        )

    def relay(self):
        self.across().wait_recv()
        self.far_x().start()

    def finish(self, dst):
        at = self.at
        self.near_x().wait_recv()
        self.far_x().wait_recv()
        for x, group, spot in (
            (at.x, at.group, self.result.at[0]),
            (1 - at.x, at.group, self.result.at[2]),
            (at.x, 1 - at.group, self.cross),
            (1 - at.x, 1 - at.group, self.result.at[3]),
        ):
            dst[aligned(x, self.half), aligned(group, CH)] = spot[...].astype(f32)
        self.near_x().wait_send()
        self.across().wait_send()
        self.far_x().wait_send()

    def sent(self):
        def one(j, carry):
            self.core(j).wait_send()
            for h in range(2):
                copy, away = self.out(j, h)
                pl.when(away)(copy.wait_send)
            return carry

        lax.fori_loop(0, 8, one, 0)


def cube_kernel(
    sz, images, cot, w4_in, w5_in, bias_in, masks, out, igrad, dw4, dw5, db, *scratch,
):
    bufs = scratch[:12]
    (w4, w5, part5, ebuf, fbuf, total, result, cross, bias, dbias, dsum,
     local_sem, gather_send, gather_recv, gather_core, core_send, core_recv, far_send, far_recv,
     end_send, end_recv, bias_send, bias_recv, db_send, db_recv, free_core, free_far) = scratch[12:]
    at = Place()
    work = Work(sz, images, cot, masks, out, igrad, bufs)
    gather = [
        Gather(at, given, full, local_sem.at[n], gather_send.at[n], gather_recv.at[n], gather_core.at[n])
        for n, (given, full) in enumerate(((w4_in, w4), (w5_in, w5)))
    ]
    sems = [
        (core_send.at[n], core_recv.at[n], far_send.at[n], far_recv.at[n], end_send.at[n], end_recv.at[n])
        for n in range(2)
    ]
    scatter5 = Scatter(at, part5, ebuf, fbuf, total, result, cross.at[0], sems[0])
    scatter4 = Scatter(at, w5, ebuf, fbuf, total, result, cross.at[1], sems[1])
    core = at.device(c=1 - at.c)

    barrier = pltpu.get_barrier_semaphore()

    def others(act):
        def one(m, carry):
            pl.when(m != at.number)(lambda: act(m))
            return carry

        lax.fori_loop(0, 8, one, 0)

    others(lambda m: pl.semaphore_signal(barrier, inc=1, device_id=at.cube(m), device_id_type=MESH))
    for device in (core, at.device(z=at.z2)):
        pl.semaphore_signal(barrier, inc=1, device_id=device, device_id_type=MESH)
    pl.semaphore_wait(barrier, 9)

    work.fetch_two(images)
    gather[0].begin()

    swap = remote(bias_in, bias.at[1], bias_send.at[0], bias_recv.at[0], core)
    swap.start()
    work.clear()
    work.prepare_pairs(0, 2)
    gather[0].part_a(1)
    gather[0].part_a(2)
    swap.wait_recv()
    slot = 2 + 2 * at.y + at.low
    bias[slot] = bias_in[...] + bias[1]

    def bias_way(n):
        y, z = ((1 - at.y, at.z), (at.y, at.z1), (1 - at.y, at.z1))[n]
        return remote(
            bias.at[slot], bias.at[slot], bias_send.at[1 + n], bias_recv.at[1 + n], at.device(y=y, z=z)
        )

    def bias_from(n):
        y, low = ((1 - at.y, at.low), (at.y, 1 - at.low), (1 - at.y, 1 - at.low))[n]
        spot = bias.at[2 + 2 * y + low]
        return remote(spot, spot, bias_send.at[1 + n], bias_recv.at[1 + n], core)

    for n in range(3):
        bias_way(n).start()
    gather[0].part_b(1)
    work.prepare_pairs(2, 4)
    gather[0].part_a(3)
    gather[0].part_b(2)
    work.prepare_pairs(4, 6)
    work.prepare(12, 0)
    work.fetch_end(images)
    work.fetch_two(cot)
    gather[0].part_b(3)
    for n in range(3):
        bias_from(n).wait_recv()
    gather[0].near()

    def far_steps(n, t):
        one = gather[n]

        def at_step(k, *acts):
            @pl.when(t == k)
            def _():
                for act, arg in acts:
                    act(arg)

        at_step(0, (one.part_a, 4), (one.part_b, 4))
        at_step(1, (one.part_a, 5))
        at_step(2, (one.part_b, 5))
        at_step(3, (one.part_a, 6))
        at_step(4, (one.part_b, 6), (one.part_a, 7))

    def near_steps(n, t):
        one = gather[n]

        def at_step(k, *acts):
            @pl.when(t == k)
            def _():
                for act, arg in acts:
                    act(arg)

        at_step(0, (one.part_a, 1), (one.part_a, 2))
        at_step(1, (one.part_b, 1))
        at_step(2, (one.part_a, 3))
        at_step(3, (one.part_b, 2))
        at_step(4, (one.part_b, 3))

    rows = sz.rows
    near_tap, far_tap = at.group * 5, (1 - at.group) * 4

    def store4(i, value):
        work.pre4[aligned(i, rows), :] = value

    work.partial_rows(work.conv_taps(work.pbuf, w4, near_tap, 4), store4, functools.partial(far_steps, 0))
    gather[0].part_b(7)
    gather[1].begin()
    gather[0].far()

    def rest4(i, skip=None):
        return work.conv_taps(work.pbuf, w4, far_tap, 5)(i) + work.pre4[aligned(i, rows), :]

    def bias_rows(n):
        return jnp.concatenate([bias[2 + m, n : n + 1, :] for m in (0, 2, 1, 3)], 1)

    work.rows13(rest4, work.finish4(bias_rows(0)), functools.partial(near_steps, 1))
    gather[1].near()

    def store5(i, value):
        high = value.astype(bf16)
        where = aligned(i + 1, rows)
        work.pbuf[where, 0:CH] = high
        work.pbuf[where, CH : 2 * CH] = (value - high.astype(f32)).astype(bf16)

    work.partial_rows(work.conv_taps(work.qbuf, w5, near_tap, 4), store5, functools.partial(far_steps, 1))
    gather[1].part_b(7)
    gather[1].far()

    def rest5(i, skip=None):
        where = aligned(i + 1, rows)
        kept = work.pbuf[where, 0:CH].astype(f32) + work.pbuf[where, CH : 2 * CH].astype(f32)
        return work.conv_taps(work.qbuf, w5, far_tap, 5)(i) + kept

    work.put_two(out)
    dbias[...] = jnp.zeros_like(dbias)
    db4, db5 = dbias.at[0, 0:8], dbias.at[0, 8:16]
    work.rows13(rest5, work.finish5(bias_rows(1), db5))
    work.fetch_end(cot)
    for one in gather:
        one.sent()
    swap.wait_send()
    for n in range(3):
        bias_way(n).wait_send()

    work.wgrad(work.ht, work.pbuf, part5, scatter5.tap)
    scatter5.take(7)
    pl.semaphore_signal(free_core, inc=1, device_id=core, device_id_type=MESH)

    def end_steps(one, t):
        @pl.when(t == 4)
        def _():
            one.sum_far()

        @pl.when(t == 6)
        def _():
            one.relay()

    work.rows13(work.back(work.pbuf, w5), work.finish_back5(db4), functools.partial(end_steps, scatter5))
    others(lambda m: pl.semaphore_signal(free_far, inc=1, device_id=at.cube(m), device_id_type=MESH))
    scatter5.finish(dw5)
    scatter5.sent()

    db_swap = remote(dbias.at[0], dbias.at[1], db_send.at[8], db_recv.at[8], core)
    db_swap.start()

    def db_way(m):
        return remote(dsum.at[at.number], dsum.at[at.number], db_send.at[m], db_recv.at[at.number], at.cube(m))

    def db_from(m):
        return remote(dsum.at[m], dsum.at[m], db_send.at[m], db_recv.at[m], at.cube(m))

    def tap4(t):
        @pl.when(t == 1)
        def _():
            pl.semaphore_wait(free_core, 1)

        @pl.when(t == 2)
        def _():
            pl.semaphore_wait(free_far, 7)

        @pl.when(t == 4)
        def _():
            db_swap.wait_recv()
            dsum[at.number] = dbias[0] + dbias[1]
            others(lambda m: db_way(m).start())

        scatter4.tap(t)

    work.wgrad(work.xt, work.qbuf, w5, tap4)
    scatter4.take(7)

    work.put_end(out)
    work.put_two(igrad)
    work.rows13(
        work.back(work.qbuf, w4), work.finish_back4, functools.partial(end_steps, scatter4)
    )
    others(lambda m: db_from(m).wait_recv())
    whole = dsum[0]
    for m in range(1, 8):
        whole = whole + dsum[m]
    db[0:1, :] = jnp.sum(whole[0:8], axis=0, keepdims=True)
    db[1:2, :] = jnp.sum(whole[8:16], axis=0, keepdims=True)
    db_swap.wait_send()
    others(lambda m: db_way(m).wait_send())
    work.put_end(igrad)
    scatter4.finish(dw4)
    scatter4.sent()


def cube_shards(images, conv4_weight, conv4_bias, conv5_weight, conv5_bias, cotangent):
    sz = Sizes(images.shape[0])
    size = conv4_weight.shape[0]
    stream = lax.axis_index("stream")
    pair = jnp.stack([conv4_bias, conv5_bias]).astype(f32)
    width = conv4_bias.shape[0]
    pair = jnp.pad(pair, ((0, 6), (0, 0)))
    blank = jnp.zeros_like(pair)
    pair = jnp.where(
        stream % 2 == 0, jnp.concatenate([pair, blank], 1), jnp.concatenate([blank, pair], 1)
    )
    vm = pl.BlockSpec(memory_space=pltpu.VMEM)
    hb = pl.BlockSpec(memory_space=pl.ANY)
    dma = pltpu.SemaphoreType.DMA
    out, igrad, dw4, dw5, db = pl.pallas_call(
        functools.partial(cube_kernel, sz),
        out_shape=(
            jax.ShapeDtypeStruct(images.shape, bf16),
            jax.ShapeDtypeStruct(images.shape, bf16),
            jax.ShapeDtypeStruct((size, 2 * CH), f32),
            jax.ShapeDtypeStruct((size, 2 * CH), f32),
            jax.ShapeDtypeStruct((2, CH), f32),
        ),
        in_specs=[hb, hb, hb, hb, vm, vm],
        out_specs=(hb, hb, vm, vm, vm),
        scratch_shapes=Work.buffers(sz)
        + [
            pltpu.VMEM((TAPS * CH, CH), bf16),
            pltpu.VMEM((TAPS * CH, CH), bf16),
            pltpu.VMEM((TAPS * CH, CH), bf16),
            pltpu.VMEM((8, size, CH), bf16),
            pltpu.VMEM((2, 8, size // 2, CH), bf16),
            pltpu.VMEM((2, size // 2, CH), f32),
            pltpu.VMEM((4, size // 2, CH), bf16),
            pltpu.VMEM((2, size // 2, CH), bf16),
            pltpu.VMEM((6, 8, 2 * width), f32),
            pltpu.VMEM((2, 16, CH), f32),
            pltpu.VMEM((8, 16, CH), f32),
            dma((2,)),
            dma((2, Gather.SENDS)),
            dma((2, 8, 2)),
            dma((2, 8)),
            dma((2, 8)),
            dma((2, 8)),
            dma((2, 8, 2)),
            dma((2, 2, 8)),
            dma((2, 3)),
            dma((2, 3)),
            dma((4,)),
            dma((4,)),
            dma((9,)),
            dma((9,)),
            pltpu.SemaphoreType.REGULAR,
            pltpu.SemaphoreType.REGULAR,
        ],
        compiler_params=pltpu.CompilerParams(
            vmem_limit_bytes=VMEM_LIMIT, collective_id=0, has_side_effects=True
        ),
    )(images, cotangent, conv4_weight, conv5_weight, pair, mask_rows(sz))
    own = lax.dynamic_slice_in_dim(db, stream * width % CH, width, 1)
    return out, igrad, dw4, own[0], dw5, own[1]


def solution(mesh):
    clip = P(("stream", "batch"), None, None, None)
    weight = P("stream", None)
    bias = P("stream")
    cube = dict(mesh.shape) == {"stream": 16, "batch": 2}
    return jax.shard_map(
        cube_shards if cube else plain_shards,
        mesh=mesh,
        in_specs=(clip, weight, bias, weight, bias, clip),
        out_specs=(clip, clip, weight, bias, weight, bias),
        check_vma=False,
    )
```

```python
import functools
import jax
import jax.numpy as jnp
import numpy as np
from jax import lax
from jax.experimental import pallas as pl
from jax.experimental.pallas import tpu as pltpu
from jax.sharding import PartitionSpec as P

CH = 512
SIDE = 13
TAPS = 9
ROOT = 0.7978845608
CUBE = 0.044715
VMEM_LIMIT = 64 << 20
f32 = jnp.float32
bf16 = jnp.bfloat16
MESH = pl.DeviceIdType.MESH


def tanh_part(v, v2):
    return jnp.tanh(v * (ROOT + (ROOT * CUBE) * v2))


def gelu(v):
    half = 0.5 * v
    return half + half * tanh_part(v, v * v)


def gelu_both(v):
    v2 = v * v
    t = tanh_part(v, v2)
    half = 0.5 * v
    value = half + half * t
    slope = 0.5 + 0.5 * t + half * (1.0 - t * t) * (ROOT + (3 * ROOT * CUBE) * v2)
    return value, slope


class Sizes:
    def __init__(self, clips):
        self.clips = clips
        self.used = clips * SIDE
        self.rows = -(-self.used // 16) * 16
        self.lanes = -(-self.rows // 256) * 256
        self.tall = 15 * self.rows + self.lanes - self.rows


def mask_rows(sz):
    row = np.arange(sz.rows)
    col = row % SIDE
    keep = row < sz.used
    table = np.stack([keep & (col != 0), keep, keep & (col != SIDE - 1)])
    return jnp.asarray(np.broadcast_to(table[:, :, None], (3, sz.rows, 128)), f32)


def aligned(index, size):
    return pl.ds(pl.multiple_of(index * size, size), size)


def flatten(sz, flat, stage):
    for n in range(sz.clips):
        flat[n * SIDE : (n + 1) * SIDE, :] = stage[n].astype(f32)


def unflatten(sz, stage, flat):
    for n in range(sz.clips):
        stage[n] = flat[n * SIDE : (n + 1) * SIDE, :].astype(bf16)


def fold8(value):
    return jnp.sum(value.reshape(value.shape[0] // 8, 8, CH), axis=0)


def nothing(step):
    return None


class Work:
    def __init__(self, sz, images, cot, masks, out, igrad, bufs):
        self.sz = sz
        self.images, self.cot, self.out, self.igrad = images, cot, out, igrad
        self.masks = masks
        (self.pbuf, self.qbuf, self.xt, self.ht, self.pre4, acc0, acc1, self.flat_in,
         self.stage_in, self.stage_out, self.in_sem, self.out_sem) = bufs
        self.accs = (acc0, acc1)

    @staticmethod
    def buffers(sz):
        rows, lanes = sz.rows, sz.lanes
        return [
            pltpu.VMEM((sz.tall, 3 * CH), bf16),
            pltpu.VMEM((sz.tall, 3 * CH), bf16),
            pltpu.VMEM((CH, SIDE * lanes), bf16),
            pltpu.VMEM((CH, SIDE * lanes), bf16),
            pltpu.VMEM((SIDE * rows, CH), f32),
            pltpu.VMEM((rows, CH), f32),
            pltpu.VMEM((rows, CH), f32),
            pltpu.VMEM((2, rows, CH), f32),
            pltpu.VMEM((2, sz.clips, SIDE, CH), bf16),
            pltpu.VMEM((2, sz.clips, SIDE, CH), bf16),
            pltpu.SemaphoreType.DMA((2,)),
            pltpu.SemaphoreType.DMA((2,)),
        ]

    def clear(self):
        sz, rows = self.sz, self.sz.rows
        for buf in (self.pbuf, self.qbuf):
            buf[0:rows, :] = jnp.zeros((rows, 3 * CH), bf16)
            buf[14 * rows : sz.tall, :] = jnp.zeros((sz.tall - 14 * rows, 3 * CH), bf16)
        self.flat_in[...] = jnp.zeros_like(self.flat_in)

    def fetch(self, src, i, slot):
        return pltpu.make_async_copy(src.at[:, i], self.stage_in.at[slot], self.in_sem.at[slot])

    def put(self, dst, i, slot):
        return pltpu.make_async_copy(self.stage_out.at[slot], dst.at[:, i], self.out_sem.at[slot])

    def fetch_two(self, src):
        self.fetch(src, 0, 0).start()
        self.fetch(src, 1, 1).start()

    def fetch_end(self, src):
        self.fetch(src, 12, 1).wait()
        self.fetch(src, 12, 0).wait()

    def put_two(self, dst):
        self.put(dst, 0, 0).start()
        self.put(dst, 1, 1).start()

    def put_end(self, dst):
        self.put(dst, 12, 1).wait()
        self.put(dst, 12, 0).wait()

    def spread(self, dst, block, value, flip=False):
        low, high = (2 * CH, 0) if flip else (0, 2 * CH)
        where = aligned(block, self.sz.rows)
        for lane in range(0, CH, 128):
            x = value[:, lane : lane + 128]
            left = pltpu.roll(x, 1, 0) * self.masks[0]
            right = pltpu.roll(x, self.sz.rows - 1, 0) * self.masks[2]
            dst[where, low + lane : low + lane + 128] = left.astype(bf16)
            dst[where, CH + lane : CH + lane + 128] = (x * self.masks[1]).astype(bf16)
            dst[where, high + lane : high + lane + 128] = right.astype(bf16)

    def kept(self, value):
        return jnp.concatenate([value[:, k : k + 128] * self.masks[1] for k in range(0, CH, 128)], 1)

    def turn(self, dst, i, value):
        sz = self.sz
        blank = jnp.zeros((sz.lanes - sz.rows, CH), f32)
        full = jnp.concatenate([self.kept(value), blank], 0).astype(bf16)
        dst[:, aligned(i, sz.lanes)] = full.T

    def prepare(self, i, slot):
        self.fetch(self.images, i, slot).wait()
        flatten(self.sz, self.flat_in.at[slot], self.stage_in.at[slot])
        self.fetch(self.images, jnp.minimum(i + 2, 12), slot).start()
        value = self.flat_in[slot]
        self.spread(self.pbuf, i + 1, value)
        self.turn(self.xt, i, value)

    def prepare_pairs(self, first, last):
        def pair(t, carry):
            self.prepare(2 * t, 0)
            self.prepare(2 * t + 1, 1)
            return carry

        lax.fori_loop(first, last, pair, 0)

    def rows13(self, product, finish, service=nothing):
        accs = self.accs
        accs[0][...] = product(0, 0)

        def pair(t, carry):
            i = 2 * t
            service(t)
            accs[1][...] = product(i + 1)
            finish(i, accs[0], 0)
            accs[0][...] = product(i + 2)
            finish(i + 1, accs[1], 1)
            return carry

        lax.fori_loop(0, 5, pair, 0)
        service(5)
        accs[1][...] = product(11)
        finish(10, accs[0], 0)
        service(6)
        accs[0][...] = product(12, 2)
        finish(11, accs[1], 1)
        finish(12, accs[0], 0)

    def conv(self, src, w):
        rows = self.sz.rows

        def product(i, skip=None):
            total = None
            for a in range(3):
                if a == skip:
                    continue
                term = jnp.dot(
                    src[aligned(i + a, rows), :],
                    w[a * 3 * CH : (a + 1) * 3 * CH, :],
                    preferred_element_type=f32,
                )
                total = term if total is None else total + term
            return total

        return product

    def back(self, src, w):
        rows = self.sz.rows

        def product(i, skip=None):
            total = None
            for a in range(3):
                if skip is not None and a == 2 - skip:
                    continue
                term = jnp.dot(
                    src[aligned(i + 2 - a, rows), :],
                    w[a * 3 * CH : (a + 1) * 3 * CH, :],
                    preferred_element_type=f32,
                )
                total = term if total is None else total + term
            return total

        return product

    def wgrad(self, left, src, w, dst, flip=None, service=nothing):
        rows, lanes = self.sz.rows, self.sz.lanes

        def one(t, carry):
            tap = t if flip is None else t + flip * (TAPS - 1 - 2 * t)
            a, b = tap // 3, tap % 3
            total = None
            for q in range(13):
                start = pl.multiple_of((q + 2 - a) * rows, 16)
                term = jnp.dot(
                    left[:, q * lanes : (q + 1) * lanes],
                    src[pl.ds(start, lanes), aligned(b, CH)],
                    preferred_element_type=f32,
                )
                total = term if total is None else total + term
            w[aligned(tap, CH), :] = w[aligned(tap, CH), :].T
            dst[aligned(tap, CH), :] = total.astype(dst.dtype)
            service(t)
            return carry

        lax.fori_loop(0, TAPS, one, 0)

    def finish4(self, b4):
        def finish(i, acc, slot):
            v = acc[...] + b4
            self.pre4[aligned(i, self.sz.rows), :] = v
            h = gelu(v)
            self.spread(self.qbuf, i + 1, h)
            self.turn(self.ht, i, h)

        return finish

    def finish5(self, b5, db5):
        def finish(i, acc, slot):
            self.put(self.out, i, slot).wait()
            self.fetch(self.cot, i, slot).wait()
            flatten(self.sz, self.flat_in.at[slot], self.stage_in.at[slot])
            self.fetch(self.cot, jnp.minimum(i + 2, 12), slot).start()
            value, slope = gelu_both(acc[...] + b5)
            acc[...] = value
            unflatten(self.sz, self.stage_out.at[slot], acc)
            self.put(self.out, i, slot).start()
            g = (self.flat_in[slot] * slope).astype(bf16).astype(f32)
            db5[...] += fold8(g)
            self.spread(self.pbuf, i + 1, g, True)

        return finish

    def finish_back5(self, db4):
        def finish(i, acc, slot):
            g = acc[...] * gelu_both(self.pre4[aligned(i, self.sz.rows), :])[1]
            g = self.kept(g).astype(bf16).astype(f32)
            db4[...] += fold8(g)
            self.spread(self.qbuf, i + 1, g, True)

        return finish

    def finish_back4(self, i, acc, slot):
        self.put(self.igrad, i, slot).wait()
        unflatten(self.sz, self.stage_out.at[slot], acc)
        self.put(self.igrad, i, slot).start()


def alone_kernel(
    sz, images, cot, w4_in, w5_in, b4, b5, masks, out, igrad, dw4, dw5, db4, db5, *scratch,
):
    bufs, (w4, w5, sems) = scratch[:12], scratch[12:]
    loads = [
        pltpu.make_async_copy(src, dst, sems.at[n])
        for n, (src, dst) in enumerate(((w4_in, w4), (w5_in, w5)))
    ]
    for load in loads:
        load.start()
    work = Work(sz, images, cot, masks, out, igrad, bufs)
    work.clear()
    work.fetch_two(images)
    work.prepare_pairs(0, 6)
    work.prepare(12, 0)
    work.fetch_end(images)
    work.fetch_two(cot)
    for load in loads:
        load.wait()
    work.rows13(work.conv(work.pbuf, w4), work.finish4(b4[...]))
    work.put_two(out)
    db5[...] = jnp.zeros_like(db5)
    work.rows13(work.conv(work.qbuf, w5), work.finish5(b5[...], db5))
    work.fetch_end(cot)
    work.wgrad(work.ht, work.pbuf, w5, dw5)
    db4[...] = jnp.zeros_like(db4)
    work.rows13(work.back(work.pbuf, w5), work.finish_back5(db4))
    work.wgrad(work.xt, work.qbuf, w4, dw4)
    work.put_end(out)
    work.put_two(igrad)
    work.rows13(work.back(work.qbuf, w4), work.finish_back4)
    work.put_end(igrad)


def block(images, cot, w4, w5, b4, b5):
    sz = Sizes(images.shape[0])
    vm = pl.BlockSpec(memory_space=pltpu.VMEM)
    hb = pl.BlockSpec(memory_space=pl.ANY)
    return pl.pallas_call(
        functools.partial(alone_kernel, sz),
        out_shape=(
            jax.ShapeDtypeStruct(images.shape, bf16),
            jax.ShapeDtypeStruct(images.shape, bf16),
            jax.ShapeDtypeStruct((TAPS * CH, CH), bf16),
            jax.ShapeDtypeStruct((TAPS * CH, CH), bf16),
            jax.ShapeDtypeStruct((8, CH), f32),
            jax.ShapeDtypeStruct((8, CH), f32),
        ),
        in_specs=[hb, hb, hb, hb, vm, vm, vm],
        out_specs=(hb, hb, vm, vm, vm, vm),
        scratch_shapes=Work.buffers(sz)
        + [
            pltpu.VMEM((TAPS * CH, CH), bf16),
            pltpu.VMEM((TAPS * CH, CH), bf16),
            pltpu.SemaphoreType.DMA((2,)),
        ],
        compiler_params=pltpu.CompilerParams(vmem_limit_bytes=VMEM_LIMIT),
    )(images, cot, w4, w5, b4.reshape(1, CH).astype(f32), b5.reshape(1, CH).astype(f32), mask_rows(sz))


def plain_shards(images, conv4_weight, conv4_bias, conv5_weight, conv5_bias, cotangent):
    half = lax.axis_size("stream") // 2
    group = lax.axis_index("stream") // half
    weights = lax.all_gather(
        jnp.concatenate([conv4_weight, conv5_weight], 1), "stream", axis=0, tiled=True
    )
    biases = lax.all_gather(jnp.stack([conv4_bias, conv5_bias], 1), "stream", axis=0, tiled=True)
    w4 = lax.dynamic_slice_in_dim(weights, group * CH, CH, 1)
    w5 = lax.dynamic_slice_in_dim(weights, (group + 2) * CH, CH, 1)
    own = lax.dynamic_slice_in_dim(biases, group * CH, CH, 0)
    out, igrad, dw4, dw5, db4, db5 = block(images, cotangent, w4, w5, own[:, 0], own[:, 1])

    def widen(value):
        value = value.astype(f32)
        blank = jnp.zeros_like(value)
        return jnp.where(
            group == 0,
            jnp.concatenate([value, blank], -1),
            jnp.concatenate([blank, value], -1),
        )

    def reduce(value):
        value = lax.psum_scatter(widen(value), "stream", scatter_dimension=0, tiled=True)
        return lax.psum(value.astype(bf16), "batch").astype(f32)

    dw4, dw5 = reduce(dw4), reduce(dw5)
    db = lax.psum(jnp.stack([widen(db4.sum(0)), widen(db5.sum(0))]), ("stream", "batch"))
    size = conv4_bias.shape[0]
    db = lax.dynamic_slice_in_dim(db, lax.axis_index("stream") * size, size, 1)
    return out, igrad, dw4, db[0], dw5, db[1]


class Place:
    def __init__(self):
        s = lax.axis_index("stream")
        self.x = lax.axis_index("batch")
        self.c = s % 2
        self.y = (s // 2) % 2
        self.z = s // 4
        self.low = self.z % 2
        self.group = self.z // 2
        self.z1 = self.z + 1 - 2 * self.low
        self.z2 = (self.z + 2) % 4
        self.z12 = (self.z1 + 2) % 4
        self.number = self.x * 4 + self.y * 2 + self.low
        self.lead = self.c == self.x

    def device(self, x=None, y=None, z=None, c=None):
        x = self.x if x is None else x
        y = self.y if y is None else y
        z = self.z if z is None else z
        c = self.c if c is None else c
        return {"stream": (z * 2 + y) * 2 + c, "batch": x}

    def shard(self, k, c):
        z = (self.z, self.z1, self.z, self.z1, self.z2, self.z12, self.z2, self.z12)[k]
        y = self.y if k in (0, 1, 4, 5) else 1 - self.y
        return (z * 2 + y) * 2 + c

    def cube(self, m):
        return self.device(x=m // 4, y=(m // 2) % 2, z=self.group * 2 + m % 2)


def remote(src, dst, send, recv, device):
    return pltpu.make_async_remote_copy(
        src_ref=src, dst_ref=dst, send_sem=send, recv_sem=recv, device_id=device, device_id_type=MESH
    )


class Gather:
    SENDS = 29

    def __init__(self, at, given, full, sem_local, sends, recvs, cores):
        self.at, self.given, self.full = at, given, full
        self.sem_local, self.sends, self.recvs, self.cores = sem_local, sends, recvs, cores
        self.size = given.shape[0]
        self.cut = self.size * 2 // 7 // 16 * 16

    def rows(self, shard, part):
        start = (0, self.cut, 0)[part]
        size = (self.cut, self.size - self.cut, self.size)[part]
        return pl.ds(pl.multiple_of(shard * self.size + start, 16), size)

    def mine(self, part, group):
        start = (0, self.cut, 0)[part]
        size = (self.cut, self.size - self.cut, self.size)[part]
        return self.given.at[pl.ds(start, size), aligned(group, CH)]

    def ring(self, k):
        at = self.at
        ways = (at.device(y=1 - at.y, z=at.z1), at.device(z=at.z1), at.device(y=1 - at.y))
        return [
            (k + there, device, 2 + 2 * k // 4 * 3 + 2 * n)
            for n, (there, device) in enumerate(zip((3, 1, 2), ways))
        ]

    def copies(self, k, part):
        at = self.at
        spot = self.full.at[self.rows(at.shard(k, at.c), part), :]
        src = self.mine(part, at.group) if k == 0 else spot
        made = []
        if k == 0:
            made.append(
                remote(
                    self.mine(part, 1 - at.group), spot,
                    self.sends.at[part], self.recvs.at[4, part], at.device(z=at.z2),
                )
            )
        if k in (0, 4):
            made += [
                remote(src, spot, self.sends.at[slot + part], self.recvs.at[there, part], device)
                for there, device, slot in self.ring(k)
            ]
        if k > 0 and part == 1:
            made.append(
                remote(spot, spot, self.sends.at[13 + k], self.recvs.at[k, 1], at.device(x=1 - at.x))
            )
        return made

    def core(self, k):
        at = self.at
        spot = self.full.at[self.rows(at.shard(k, at.c), 2), :]
        src = self.mine(2, at.group) if k == 0 else spot
        return remote(src, spot, self.sends.at[21 + k], self.cores.at[k], at.device(c=1 - at.c))

    def local(self):
        at = self.at
        spot = self.full.at[self.rows(at.shard(0, at.c), 2), :]
        return pltpu.make_async_copy(self.mine(2, at.group), spot, self.sem_local)

    def begin(self):
        for copy in self.copies(0, 0):
            copy.start()

        @pl.when(self.at.lead)
        def _():
            for copy in self.copies(0, 1):
                copy.start()

        self.core(0).start()
        self.local().start()

    def arrived(self, k, part):
        at = self.at
        spot = self.full.at[self.rows(at.shard(k, at.c), part), :]
        return remote(spot, spot, self.sends.at[0], self.recvs.at[k, part], at.device(c=1 - at.c))

    def first(self, k):
        self.arrived(k, 0).wait_recv()
        for copy in self.copies(k, 0):
            copy.start()

    def rest(self, k):
        self.lead(k)
        self.follow(k)

    def landed(self, k):
        if k != 4:
            self.arrived(k, 0).wait_recv()
        self.arrived(k, 1).wait_recv()

    def lead(self, k):
        @pl.when(self.at.lead)
        def _():
            self.landed(k)
            for copy in self.copies(k, 1):
                copy.start()
            self.core(k).start()

    def follow(self, k):
        @pl.when(jnp.logical_not(self.at.lead))
        def _():
            self.landed(k)
            self.core(k).start()

    def from_core(self, k):
        at = self.at
        spot = self.full.at[self.rows(at.shard(k, 1 - at.c), 2), :]
        remote(spot, spot, self.sends.at[0], self.cores.at[k], at.device(c=1 - at.c)).wait_recv()

    def whole(self):
        self.local().wait()
        for k in range(8):
            self.from_core(k)

    def sent(self):
        for k in range(8):
            for copy in self.copies(k, 0):
                copy.wait_send()
            self.core(k).wait_send()

        @pl.when(self.at.lead)
        def _():
            for k in range(8):
                for copy in self.copies(k, 1):
                    copy.wait_send()


class Scatter:
    def __init__(self, at, part, ebuf, fbuf, total, result, cross, sems):
        self.at, self.part, self.ebuf, self.fbuf, self.total, self.result = at, part, ebuf, fbuf, total, result
        self.cross = cross
        self.core_send, self.core_recv, self.far_send, self.far_recv, self.end_send, self.end_recv = sems
        self.size = ebuf.shape[1]
        self.flip = 1 - at.group
        self.half = self.size // 2

    def pair(self, n):
        return n + self.flip * (7 - 2 * n)

    def shard(self, j, c):
        return self.part.at[pl.ds(pl.multiple_of((2 * j + c) * self.size, 16), self.size), :]

    def core(self, j):
        at = self.at
        return remote(
            self.shard(j, 1 - at.c), self.ebuf.at[j], self.core_send.at[j], self.core_recv.at[j],
            at.device(c=1 - at.c),
        )

    def give(self, n):
        self.core(self.pair(n)).start()

    def out(self, j, h):
        at = self.at
        z, y = j // 2, j % 2
        to_z = at.group * 2 + z % 2
        kind = (z // 2 + at.group) % 2
        start = pl.multiple_of((2 * j + at.c) * self.size + h * self.half, 16)
        copy = remote(
            self.part.at[pl.ds(start, self.half), :], self.fbuf.at[kind, at.number],
            self.far_send.at[j, h], self.far_recv.at[kind, at.number],
            at.device(x=h, y=y, z=to_z),
        )
        away = (at.x + 2 * at.y + 4 * at.z) != (h + 2 * y + 4 * to_z)
        return copy, away

    def take(self, n):
        at = self.at
        j = self.pair(n)
        self.core(j).wait_recv()
        start = pl.multiple_of((2 * j + at.c) * self.size, 16)
        where = pl.ds(start, self.size)
        self.part[where, :] = (self.part[where, :].astype(f32) + self.ebuf[j].astype(f32)).astype(bf16)
        for h in range(2):
            copy, away = self.out(j, h)
            pl.when(away)(copy.start)

    def tap(self, t):
        @pl.when(t >= 1)
        def _():
            self.give(t - 1)

        @pl.when(t >= 2)
        def _():
            self.take(t - 2)

    def sum_far(self, kind):
        at = self.at
        z = at.z if kind == 0 else at.z2
        start = pl.multiple_of(((z * 2 + at.y) * 2 + at.c) * self.size + at.x * self.half, 16)
        self.total[...] = self.part[pl.ds(start, self.half), :].astype(f32)

        def add(m, carry):
            @pl.when(m != at.number)
            def _():
                spot = self.fbuf.at[kind, m]
                remote(
                    spot, spot, self.far_send.at[0, 0], self.far_recv.at[kind, m], at.device(c=1 - at.c)
                ).wait_recv()
                self.total[...] += spot[...].astype(f32)

            return carry

        lax.fori_loop(0, 8, add, 0)
        self.result[kind] = self.total[...].astype(bf16)
        if kind == 0:
            self.near_x().start()
        else:
            self.across().start()

    def near_x(self):
        at = self.at
        return remote(
            self.result.at[0], self.result.at[2], self.end_send.at[0], self.end_recv.at[0], at.device(x=1 - at.x)
        )

    def across(self):
        at = self.at
        return remote(
            self.result.at[1], self.cross, self.end_send.at[1], self.end_recv.at[1], at.device(z=at.z2)
        )

    def far_x(self):
        at = self.at
        return remote(
            self.cross, self.result.at[3], self.end_send.at[2], self.end_recv.at[2], at.device(x=1 - at.x)
        )

    def relay(self):
        self.across().wait_recv()
        self.far_x().start()

    def finish(self, dst):
        at = self.at
        self.near_x().wait_recv()
        self.far_x().wait_recv()
        for x, group, spot in (
            (at.x, at.group, self.result.at[0]),
            (1 - at.x, at.group, self.result.at[2]),
            (at.x, 1 - at.group, self.cross),
            (1 - at.x, 1 - at.group, self.result.at[3]),
        ):
            dst[aligned(x, self.half), aligned(group, CH)] = spot[...].astype(f32)
        self.near_x().wait_send()
        self.across().wait_send()
        self.far_x().wait_send()

    def sent(self):
        def one(j, carry):
            self.core(j).wait_send()
            for h in range(2):
                copy, away = self.out(j, h)
                pl.when(away)(copy.wait_send)
            return carry

        lax.fori_loop(0, 8, one, 0)


def cube_kernel(
    sz, images, cot, w4_in, w5_in, bias_in, masks, out, igrad, dw4, dw5, db, *scratch,
):
    bufs = scratch[:12]
    (w4, w5, part5, ebuf, fbuf, total, result, cross, bias, dbias, dsum,
     local_sem, gather_send, gather_recv, gather_core, core_send, core_recv, far_send, far_recv,
     end_send, end_recv, bias_send, bias_recv, db_send, db_recv, free_core, free_far) = scratch[12:]
    at = Place()
    work = Work(sz, images, cot, masks, out, igrad, bufs)
    gather = [
        Gather(at, given, full, local_sem.at[n], gather_send.at[n], gather_recv.at[n], gather_core.at[n])
        for n, (given, full) in enumerate(((w4_in, w4), (w5_in, w5)))
    ]
    sems = [
        (core_send.at[n], core_recv.at[n], far_send.at[n], far_recv.at[n], end_send.at[n], end_recv.at[n])
        for n in range(2)
    ]
    scatter5 = Scatter(at, part5, ebuf, fbuf, total, result, cross.at[0], sems[0])
    scatter4 = Scatter(at, w5, ebuf, fbuf, total, result, cross.at[1], sems[1])
    core = at.device(c=1 - at.c)

    barrier = pltpu.get_barrier_semaphore()

    def others(act):
        def one(m, carry):
            pl.when(m != at.number)(lambda: act(m))
            return carry

        lax.fori_loop(0, 8, one, 0)

    others(lambda m: pl.semaphore_signal(barrier, inc=1, device_id=at.cube(m), device_id_type=MESH))
    for device in (core, at.device(z=at.z2)):
        pl.semaphore_signal(barrier, inc=1, device_id=device, device_id_type=MESH)
    pl.semaphore_wait(barrier, 9)

    work.fetch_two(images)
    gather[0].begin()

    swap = remote(bias_in, bias.at[1], bias_send.at[0], bias_recv.at[0], core)
    swap.start()
    work.clear()
    work.prepare_pairs(0, 2)
    gather[0].first(4)
    swap.wait_recv()
    slot = 2 + 2 * at.y + at.low
    bias[slot] = bias_in[...] + bias[1]

    def bias_way(n):
        y, z = ((1 - at.y, at.z), (at.y, at.z1), (1 - at.y, at.z1))[n]
        return remote(
            bias.at[slot], bias.at[slot], bias_send.at[1 + n], bias_recv.at[1 + n], at.device(y=y, z=z)
        )

    def bias_from(n):
        y, low = ((1 - at.y, at.low), (at.y, 1 - at.low), (1 - at.y, 1 - at.low))[n]
        spot = bias.at[2 + 2 * y + low]
        return remote(spot, spot, bias_send.at[1 + n], bias_recv.at[1 + n], core)

    for n in range(3):
        bias_way(n).start()
    work.prepare_pairs(2, 4)
    gather[0].rest(1)
    gather[0].rest(2)
    gather[0].rest(3)
    work.prepare_pairs(4, 6)
    work.prepare(12, 0)
    work.fetch_end(images)
    work.fetch_two(cot)
    gather[0].rest(4)
    gather[1].begin()
    for n in range(3):
        bias_from(n).wait_recv()
    for k in (5, 6, 7):
        gather[0].rest(k)
    gather[0].whole()

    def steps(plan):
        def service(t):
            for k, acts in plan.items():
                @pl.when(t == k)
                def _(acts=acts):
                    for act, *given in acts:
                        act(*given)

        return service

    def gather_plan(one):
        return steps({
            0: [(one.first, 4), (one.lead, 1), (one.lead, 2)],
            1: [(one.lead, 3), (one.follow, 1), (one.follow, 2)],
            2: [(one.lead, 4), (one.follow, 3)],
            3: [(one.lead, 5), (one.follow, 4)],
            4: [(one.lead, 6), (one.lead, 7), (one.follow, 5)],
            5: [(one.follow, 6), (one.follow, 7)],
        })

    def bias_rows(n):
        return jnp.concatenate([bias[2 + m, n : n + 1, :] for m in (0, 2, 1, 3)], 1)

    work.rows13(work.conv(work.pbuf, w4), work.finish4(bias_rows(0)), gather_plan(gather[1]))
    gather[1].whole()

    work.put_two(out)
    dbias[...] = jnp.zeros_like(dbias)
    db4, db5 = dbias.at[0, 0:8], dbias.at[0, 8:16]
    work.rows13(work.conv(work.qbuf, w5), work.finish5(bias_rows(1), db5))
    work.fetch_end(cot)
    for one in gather:
        one.sent()
    swap.wait_send()
    for n in range(3):
        bias_way(n).wait_send()

    work.wgrad(work.ht, work.pbuf, w5, part5, scatter5.flip, scatter5.tap)
    scatter5.take(7)
    pl.semaphore_signal(free_core, inc=1, device_id=core, device_id_type=MESH)

    work.rows13(
        work.back(work.pbuf, w5), work.finish_back5(db4),
        steps({2: [(scatter5.sum_far, 1)], 6: [(scatter5.sum_far, 0)]}),
    )
    others(lambda m: pl.semaphore_signal(free_far, inc=1, device_id=at.cube(m), device_id_type=MESH))
    scatter5.relay()
    scatter5.sent()

    db_swap = remote(dbias.at[0], dbias.at[1], db_send.at[8], db_recv.at[8], core)
    db_swap.start()

    def db_way(m):
        return remote(dsum.at[at.number], dsum.at[at.number], db_send.at[m], db_recv.at[at.number], at.cube(m))

    def db_from(m):
        return remote(dsum.at[m], dsum.at[m], db_send.at[m], db_recv.at[m], at.cube(m))

    def tap4(t):
        @pl.when(t == 1)
        def _():
            pl.semaphore_wait(free_core, 1)

        @pl.when(t == 2)
        def _():
            scatter5.finish(dw5)
            pl.semaphore_wait(free_far, 7)

        @pl.when(t == 4)
        def _():
            db_swap.wait_recv()
            dsum[at.number] = dbias[0] + dbias[1]
            others(lambda m: db_way(m).start())

        scatter4.tap(t)

    work.wgrad(work.xt, work.qbuf, w4, w5, scatter4.flip, tap4)
    scatter4.take(7)

    work.put_end(out)
    work.put_two(igrad)
    work.rows13(
        work.back(work.qbuf, w4), work.finish_back4,
        steps({
            2: [(scatter4.sum_far, 1)],
            4: [(scatter4.relay,)],
            5: [(scatter4.sum_far, 0)],
        }),
    )
    others(lambda m: db_from(m).wait_recv())
    whole = dsum[0]
    for m in range(1, 8):
        whole = whole + dsum[m]
    db[0:1, :] = jnp.sum(whole[0:8], axis=0, keepdims=True)
    db[1:2, :] = jnp.sum(whole[8:16], axis=0, keepdims=True)
    db_swap.wait_send()
    others(lambda m: db_way(m).wait_send())
    work.put_end(igrad)
    scatter4.finish(dw4)
    scatter4.sent()


def cube_shards(images, conv4_weight, conv4_bias, conv5_weight, conv5_bias, cotangent):
    sz = Sizes(images.shape[0])
    size = conv4_weight.shape[0]
    stream = lax.axis_index("stream")
    pair = jnp.stack([conv4_bias, conv5_bias]).astype(f32)
    width = conv4_bias.shape[0]
    pair = jnp.pad(pair, ((0, 6), (0, 0)))
    blank = jnp.zeros_like(pair)
    pair = jnp.where(
        stream % 2 == 0, jnp.concatenate([pair, blank], 1), jnp.concatenate([blank, pair], 1)
    )
    vm = pl.BlockSpec(memory_space=pltpu.VMEM)
    hb = pl.BlockSpec(memory_space=pl.ANY)
    dma = pltpu.SemaphoreType.DMA
    out, igrad, dw4, dw5, db = pl.pallas_call(
        functools.partial(cube_kernel, sz),
        out_shape=(
            jax.ShapeDtypeStruct(images.shape, bf16),
            jax.ShapeDtypeStruct(images.shape, bf16),
            jax.ShapeDtypeStruct((size, 2 * CH), f32),
            jax.ShapeDtypeStruct((size, 2 * CH), f32),
            jax.ShapeDtypeStruct((2, CH), f32),
        ),
        in_specs=[hb, hb, hb, hb, vm, vm],
        out_specs=(hb, hb, vm, vm, vm),
        scratch_shapes=Work.buffers(sz)
        + [
            pltpu.VMEM((TAPS * CH, CH), bf16),
            pltpu.VMEM((TAPS * CH, CH), bf16),
            pltpu.VMEM((TAPS * CH, CH), bf16),
            pltpu.VMEM((8, size, CH), bf16),
            pltpu.VMEM((2, 8, size // 2, CH), bf16),
            pltpu.VMEM((size // 2, CH), f32),
            pltpu.VMEM((4, size // 2, CH), bf16),
            pltpu.VMEM((2, size // 2, CH), bf16),
            pltpu.VMEM((6, 8, 2 * width), f32),
            pltpu.VMEM((2, 16, CH), f32),
            pltpu.VMEM((8, 16, CH), f32),
            dma((2,)),
            dma((2, Gather.SENDS)),
            dma((2, 8, 2)),
            dma((2, 8)),
            dma((2, 8)),
            dma((2, 8)),
            dma((2, 8, 2)),
            dma((2, 2, 8)),
            dma((2, 3)),
            dma((2, 3)),
            dma((4,)),
            dma((4,)),
            dma((9,)),
            dma((9,)),
            pltpu.SemaphoreType.REGULAR,
            pltpu.SemaphoreType.REGULAR,
        ],
        compiler_params=pltpu.CompilerParams(
            vmem_limit_bytes=VMEM_LIMIT, collective_id=0, has_side_effects=True
        ),
    )(images, cotangent, conv4_weight, conv5_weight, pair, mask_rows(sz))
    own = lax.dynamic_slice_in_dim(db, stream * width % CH, width, 1)
    return out, igrad, dw4, own[0], dw5, own[1]


def solution(mesh):
    clip = P(("stream", "batch"), None, None, None)
    weight = P("stream", None)
    bias = P("stream")
    cube = dict(mesh.shape) == {"stream": 16, "batch": 2}
    return jax.shard_map(
        cube_shards if cube else plain_shards,
        mesh=mesh,
        in_specs=(clip, weight, bias, weight, bias, clip),
        out_specs=(clip, clip, weight, bias, weight, bias),
        check_vma=False,
    )
```

```python
import functools
import jax
import jax.numpy as jnp
import numpy as np
from jax import lax
from jax.experimental import pallas as pl
from jax.experimental.pallas import tpu as pltpu
from jax.sharding import PartitionSpec as P

CH = 512
SIDE = 13
TAPS = 9
ROOT = 0.7978845608
CUBE = 0.044715
VMEM_LIMIT = 64 << 20
f32 = jnp.float32
bf16 = jnp.bfloat16
MESH = pl.DeviceIdType.MESH


def tanh_part(v, v2):
    return jnp.tanh(v * (ROOT + (ROOT * CUBE) * v2))


def gelu(v):
    half = 0.5 * v
    return half + half * tanh_part(v, v * v)


def gelu_both(v):
    v2 = v * v
    t = tanh_part(v, v2)
    half = 0.5 * v
    value = half + half * t
    slope = 0.5 + 0.5 * t + half * (1.0 - t * t) * (ROOT + (3 * ROOT * CUBE) * v2)
    return value, slope


class Sizes:
    def __init__(self, clips):
        self.clips = clips
        self.used = clips * SIDE
        self.rows = -(-self.used // 16) * 16
        self.lanes = -(-self.rows // 256) * 256
        self.tall = 15 * self.rows + self.lanes - self.rows
        self.step = 8 * max(n for n in range(1, 11) if self.rows // 8 % n == 0)


def mask_rows(sz):
    row = np.arange(sz.rows)
    col = row % SIDE
    keep = row < sz.used
    table = np.stack([keep & (col != 0), keep, keep & (col != SIDE - 1)])
    return jnp.asarray(np.broadcast_to(table[:, :, None], (3, sz.rows, 128)), f32)


def aligned(index, size):
    return pl.ds(pl.multiple_of(index * size, size), size)


def flatten(sz, flat, stage):
    for n in range(sz.clips):
        flat[n * SIDE : (n + 1) * SIDE, :] = stage[n].astype(f32)


def unflatten(sz, stage, flat):
    for n in range(sz.clips):
        stage[n] = flat[n * SIDE : (n + 1) * SIDE, :].astype(bf16)


def fold8(value):
    return jnp.sum(value.reshape(value.shape[0] // 8, 8, 128), axis=0)


def columns():
    return [slice(lane, lane + 128) for lane in range(0, CH, 128)]


def nothing(step):
    return None


class Work:
    def __init__(self, sz, images, cot, masks, out, igrad, bufs):
        self.sz = sz
        self.images, self.cot, self.out, self.igrad = images, cot, out, igrad
        self.masks = masks
        (self.pbuf, self.qbuf, self.xt, self.ht, self.pre4, acc0, acc1, self.flat_in,
         self.stage_in, self.stage_out, self.in_sem, self.out_sem) = bufs
        self.accs = (acc0, acc1)

    @staticmethod
    def buffers(sz):
        rows, lanes = sz.rows, sz.lanes
        return [
            pltpu.VMEM((sz.tall, 3 * CH), bf16),
            pltpu.VMEM((sz.tall, 3 * CH), bf16),
            pltpu.VMEM((CH, SIDE * lanes), bf16),
            pltpu.VMEM((CH, SIDE * lanes), bf16),
            pltpu.VMEM((SIDE * rows, CH), f32),
            pltpu.VMEM((rows, CH), f32),
            pltpu.VMEM((rows, CH), f32),
            pltpu.VMEM((2, rows, CH), f32),
            pltpu.VMEM((2, sz.clips, SIDE, CH), bf16),
            pltpu.VMEM((2, sz.clips, SIDE, CH), bf16),
            pltpu.SemaphoreType.DMA((2,)),
            pltpu.SemaphoreType.DMA((2,)),
        ]

    def clear(self):
        sz, rows = self.sz, self.sz.rows
        for buf in (self.pbuf, self.qbuf):
            buf[0:rows, :] = jnp.zeros((rows, 3 * CH), bf16)
            buf[14 * rows : sz.tall, :] = jnp.zeros((sz.tall - 14 * rows, 3 * CH), bf16)
        self.flat_in[...] = jnp.zeros_like(self.flat_in)

    def fetch(self, src, i, slot):
        return pltpu.make_async_copy(src.at[:, i], self.stage_in.at[slot], self.in_sem.at[slot])

    def put(self, dst, i, slot):
        return pltpu.make_async_copy(self.stage_out.at[slot], dst.at[:, i], self.out_sem.at[slot])

    def fetch_two(self, src):
        self.fetch(src, 0, 0).start()
        self.fetch(src, 1, 1).start()

    def fetch_end(self, src):
        self.fetch(src, 12, 1).wait()
        self.fetch(src, 12, 0).wait()

    def put_two(self, dst):
        self.put(dst, 0, 0).start()
        self.put(dst, 1, 1).start()

    def put_end(self, dst):
        self.put(dst, 12, 1).wait()
        self.put(dst, 12, 0).wait()

    def spread(self, dst, block, cols, x, flip=False):
        low, high = (2 * CH, 0) if flip else (0, 2 * CH)
        where, lane = aligned(block, self.sz.rows), cols.start
        left = pltpu.roll(x, 1, 0) * self.masks[0]
        right = pltpu.roll(x, self.sz.rows - 1, 0) * self.masks[2]
        dst[where, low + lane : low + lane + 128] = left.astype(bf16)
        dst[where, CH + lane : CH + lane + 128] = (x * self.masks[1]).astype(bf16)
        dst[where, high + lane : high + lane + 128] = right.astype(bf16)

    def steps(self):
        return [slice(r, r + self.sz.step) for r in range(0, self.sz.rows, self.sz.step)]

    def within(self, i, some):
        start = pl.multiple_of(i * self.sz.rows, 16) + some.start
        return pl.ds(pl.multiple_of(start, 8), self.sz.step)

    def turn(self, dst, src, i):
        sz = self.sz
        value = src[aligned(i + 1, sz.rows), CH : 2 * CH]
        blank = jnp.zeros((sz.lanes - sz.rows, CH), bf16)
        dst[:, aligned(i, sz.lanes)] = jnp.concatenate([value, blank], 0).T

    def prepare(self, i, slot):
        self.fetch(self.images, i, slot).wait()
        flatten(self.sz, self.flat_in.at[slot], self.stage_in.at[slot])
        self.fetch(self.images, jnp.minimum(i + 2, 12), slot).start()
        for cols in columns():
            self.spread(self.pbuf, i + 1, cols, self.flat_in[slot, :, cols])
        self.turn(self.xt, self.pbuf, i)

    def prepare_pairs(self, first, last):
        def pair(t, carry):
            self.prepare(2 * t, 0)
            self.prepare(2 * t + 1, 1)
            return carry

        lax.fori_loop(first, last, pair, 0)

    def rows13(self, product, finish, service=nothing):
        accs = self.accs
        accs[0][...] = product(0, 0)

        def pair(t, carry):
            i = 2 * t
            service(t)
            accs[1][...] = product(i + 1)
            finish(i, accs[0], 0)
            accs[0][...] = product(i + 2)
            finish(i + 1, accs[1], 1)
            return carry

        lax.fori_loop(0, 5, pair, 0)
        service(5)
        accs[1][...] = product(11)
        finish(10, accs[0], 0)
        service(6)
        accs[0][...] = product(12, 2)
        finish(11, accs[1], 1)
        finish(12, accs[0], 0)

    def conv(self, src, w):
        rows = self.sz.rows

        def product(i, skip=None):
            total = None
            for a in range(3):
                if a == skip:
                    continue
                term = jnp.dot(
                    src[aligned(i + a, rows), :],
                    w[a * 3 * CH : (a + 1) * 3 * CH, :],
                    preferred_element_type=f32,
                )
                total = term if total is None else total + term
            return total

        return product

    def lot(self, src, w, taps):
        rows = self.sz.rows

        def product(i, skip=None):
            total = None
            for a in taps:
                term = jnp.dot(
                    src[aligned(i + a, rows), :], w[aligned(a, 3 * CH), :], preferred_element_type=f32
                )
                total = term if total is None else total + term
            return total

        return product

    def each(self, product, store, service=nothing):
        def pair(t, carry):
            service(t)
            store(2 * t, product(2 * t))
            store(2 * t + 1, product(2 * t + 1))
            return carry

        lax.fori_loop(0, 6, pair, 0)
        store(12, product(12))

    def back(self, src, w):
        rows = self.sz.rows

        def product(i, skip=None):
            total = None
            for a in range(3):
                if skip is not None and a == 2 - skip:
                    continue
                term = jnp.dot(
                    src[aligned(i + 2 - a, rows), :],
                    w[a * 3 * CH : (a + 1) * 3 * CH, :],
                    preferred_element_type=f32,
                )
                total = term if total is None else total + term
            return total

        return product

    def wgrad(self, left, src, w, dst, flip=None, service=nothing):
        rows, lanes = self.sz.rows, self.sz.lanes

        def one(t, carry):
            tap = t if flip is None else t + flip * (TAPS - 1 - 2 * t)
            a, b = tap // 3, tap % 3
            total = None
            for q in range(13):
                start = pl.multiple_of((q + 2 - a) * rows, 16)
                term = jnp.dot(
                    left[:, q * lanes : (q + 1) * lanes],
                    src[pl.ds(start, lanes), aligned(b, CH)],
                    preferred_element_type=f32,
                )
                total = term if total is None else total + term
            w[aligned(tap, CH), :] = w[aligned(tap, CH), :].T
            dst[aligned(tap, CH), :] = total.astype(dst.dtype)
            service(t)
            return carry

        lax.fori_loop(0, TAPS, one, 0)

    def finish4(self, b4):
        def finish(i, acc, slot):
            for cols in columns():
                parts = []
                for some in self.steps():
                    v = acc[some, cols] + b4[:, cols]
                    self.pre4[self.within(i, some), cols] = v
                    parts.append(gelu(v))
                self.spread(self.qbuf, i + 1, cols, jnp.concatenate(parts, 0))
            self.turn(self.ht, self.qbuf, i)

        return finish

    def finish5(self, b5, db5):
        def finish(i, acc, slot):
            self.put(self.out, i, slot).wait()
            self.fetch(self.cot, i, slot).wait()
            flatten(self.sz, self.flat_in.at[slot], self.stage_in.at[slot])
            self.fetch(self.cot, jnp.minimum(i + 2, 12), slot).start()
            for cols in columns():
                parts, total = [], db5[:, cols]
                for some in self.steps():
                    value, slope = gelu_both(acc[some, cols] + b5[:, cols])
                    acc[some, cols] = value
                    g = (self.flat_in[slot, some, cols] * slope).astype(bf16).astype(f32)
                    total = total + fold8(g)
                    parts.append(g)
                db5[:, cols] = total
                self.spread(self.pbuf, i + 1, cols, jnp.concatenate(parts, 0), True)
            unflatten(self.sz, self.stage_out.at[slot], acc)
            self.put(self.out, i, slot).start()

        return finish

    def finish_back5(self, db4):
        def finish(i, acc, slot):
            for cols in columns():
                parts, total = [], db4[:, cols]
                for some in self.steps():
                    slope = gelu_both(self.pre4[self.within(i, some), cols])[1]
                    g = acc[some, cols] * slope * self.masks[1, some, :]
                    g = g.astype(bf16).astype(f32)
                    total = total + fold8(g)
                    parts.append(g)
                db4[:, cols] = total
                self.spread(self.qbuf, i + 1, cols, jnp.concatenate(parts, 0), True)

        return finish

    def finish_back4(self, i, acc, slot):
        self.put(self.igrad, i, slot).wait()
        unflatten(self.sz, self.stage_out.at[slot], acc)
        self.put(self.igrad, i, slot).start()


def alone_kernel(
    sz, images, cot, w4_in, w5_in, b4, b5, masks, out, igrad, dw4, dw5, db4, db5, *scratch,
):
    bufs, (w4, w5, sems) = scratch[:12], scratch[12:]
    loads = [
        pltpu.make_async_copy(src, dst, sems.at[n])
        for n, (src, dst) in enumerate(((w4_in, w4), (w5_in, w5)))
    ]
    for load in loads:
        load.start()
    work = Work(sz, images, cot, masks, out, igrad, bufs)
    work.clear()
    work.fetch_two(images)
    work.prepare_pairs(0, 6)
    work.prepare(12, 0)
    work.fetch_end(images)
    work.fetch_two(cot)
    for load in loads:
        load.wait()
    work.rows13(work.conv(work.pbuf, w4), work.finish4(b4[...]))
    work.put_two(out)
    db5[...] = jnp.zeros_like(db5)
    work.rows13(work.conv(work.qbuf, w5), work.finish5(b5[...], db5))
    work.fetch_end(cot)
    work.wgrad(work.ht, work.pbuf, w5, dw5)
    db4[...] = jnp.zeros_like(db4)
    work.rows13(work.back(work.pbuf, w5), work.finish_back5(db4))
    work.wgrad(work.xt, work.qbuf, w4, dw4)
    work.put_end(out)
    work.put_two(igrad)
    work.rows13(work.back(work.qbuf, w4), work.finish_back4)
    work.put_end(igrad)


def block(images, cot, w4, w5, b4, b5):
    sz = Sizes(images.shape[0])
    vm = pl.BlockSpec(memory_space=pltpu.VMEM)
    hb = pl.BlockSpec(memory_space=pl.ANY)
    return pl.pallas_call(
        functools.partial(alone_kernel, sz),
        out_shape=(
            jax.ShapeDtypeStruct(images.shape, bf16),
            jax.ShapeDtypeStruct(images.shape, bf16),
            jax.ShapeDtypeStruct((TAPS * CH, CH), bf16),
            jax.ShapeDtypeStruct((TAPS * CH, CH), bf16),
            jax.ShapeDtypeStruct((8, CH), f32),
            jax.ShapeDtypeStruct((8, CH), f32),
        ),
        in_specs=[hb, hb, hb, hb, vm, vm, vm],
        out_specs=(hb, hb, vm, vm, vm, vm),
        scratch_shapes=Work.buffers(sz)
        + [
            pltpu.VMEM((TAPS * CH, CH), bf16),
            pltpu.VMEM((TAPS * CH, CH), bf16),
            pltpu.SemaphoreType.DMA((2,)),
        ],
        compiler_params=pltpu.CompilerParams(vmem_limit_bytes=VMEM_LIMIT),
    )(images, cot, w4, w5, b4.reshape(1, CH).astype(f32), b5.reshape(1, CH).astype(f32), mask_rows(sz))


def plain_shards(images, conv4_weight, conv4_bias, conv5_weight, conv5_bias, cotangent):
    half = lax.axis_size("stream") // 2
    group = lax.axis_index("stream") // half
    weights = lax.all_gather(
        jnp.concatenate([conv4_weight, conv5_weight], 1), "stream", axis=0, tiled=True
    )
    biases = lax.all_gather(jnp.stack([conv4_bias, conv5_bias], 1), "stream", axis=0, tiled=True)
    w4 = lax.dynamic_slice_in_dim(weights, group * CH, CH, 1)
    w5 = lax.dynamic_slice_in_dim(weights, (group + 2) * CH, CH, 1)
    own = lax.dynamic_slice_in_dim(biases, group * CH, CH, 0)
    out, igrad, dw4, dw5, db4, db5 = block(images, cotangent, w4, w5, own[:, 0], own[:, 1])

    def widen(value):
        value = value.astype(f32)
        blank = jnp.zeros_like(value)
        return jnp.where(
            group == 0,
            jnp.concatenate([value, blank], -1),
            jnp.concatenate([blank, value], -1),
        )

    def reduce(value):
        value = lax.psum_scatter(widen(value), "stream", scatter_dimension=0, tiled=True)
        return lax.psum(value.astype(bf16), "batch").astype(f32)

    dw4, dw5 = reduce(dw4), reduce(dw5)
    db = lax.psum(jnp.stack([widen(db4.sum(0)), widen(db5.sum(0))]), ("stream", "batch"))
    size = conv4_bias.shape[0]
    db = lax.dynamic_slice_in_dim(db, lax.axis_index("stream") * size, size, 1)
    return out, igrad, dw4, db[0], dw5, db[1]


class Place:
    def __init__(self):
        s = lax.axis_index("stream")
        self.x = lax.axis_index("batch")
        self.c = s % 2
        self.y = (s // 2) % 2
        self.z = s // 4
        self.low = self.z % 2
        self.group = self.z // 2
        self.z1 = self.z + 1 - 2 * self.low
        self.z2 = (self.z + 2) % 4
        self.z12 = (self.z1 + 2) % 4
        self.number = self.x * 4 + self.y * 2 + self.low
        self.lead = self.c == self.x

    def device(self, x=None, y=None, z=None, c=None):
        x = self.x if x is None else x
        y = self.y if y is None else y
        z = self.z if z is None else z
        c = self.c if c is None else c
        return {"stream": (z * 2 + y) * 2 + c, "batch": x}

    def shard(self, k, c):
        z = (self.z, self.z1, self.z, self.z1, self.z2, self.z12, self.z2, self.z12)[k]
        y = self.y if k in (0, 1, 4, 5) else 1 - self.y
        return (z * 2 + y) * 2 + c

    def cube(self, m):
        return self.device(x=m // 4, y=(m // 2) % 2, z=self.group * 2 + m % 2)


def remote(src, dst, send, recv, device):
    return pltpu.make_async_remote_copy(
        src_ref=src, dst_ref=dst, send_sem=send, recv_sem=recv, device_id=device, device_id_type=MESH
    )


class Gather:
    SENDS = 29

    def __init__(self, at, given, full, sem_local, sends, recvs, cores):
        self.at, self.given, self.full = at, given, full
        self.sem_local, self.sends, self.recvs, self.cores = sem_local, sends, recvs, cores
        self.size = given.shape[0]
        self.cut = self.size * 2 // 7 // 16 * 16

    def rows(self, shard, part):
        start = (0, self.cut, 0)[part]
        size = (self.cut, self.size - self.cut, self.size)[part]
        return pl.ds(pl.multiple_of(shard * self.size + start, 16), size)

    def mine(self, part, group):
        start = (0, self.cut, 0)[part]
        size = (self.cut, self.size - self.cut, self.size)[part]
        return self.given.at[pl.ds(start, size), aligned(group, CH)]

    def ring(self, k):
        at = self.at
        ways = (at.device(y=1 - at.y, z=at.z1), at.device(z=at.z1), at.device(y=1 - at.y))
        return [
            (k + there, device, 2 + 2 * k // 4 * 3 + 2 * n)
            for n, (there, device) in enumerate(zip((3, 1, 2), ways))
        ]

    def copies(self, k, part):
        at = self.at
        spot = self.full.at[self.rows(at.shard(k, at.c), part), :]
        src = self.mine(part, at.group) if k == 0 else spot
        made = []
        if k == 0:
            made.append(
                remote(
                    self.mine(part, 1 - at.group), spot,
                    self.sends.at[part], self.recvs.at[4, part], at.device(z=at.z2),
                )
            )
        if k in (0, 4):
            made += [
                remote(src, spot, self.sends.at[slot + part], self.recvs.at[there, part], device)
                for there, device, slot in self.ring(k)
            ]
        if k > 0 and part == 1:
            made.append(
                remote(spot, spot, self.sends.at[13 + k], self.recvs.at[k, 1], at.device(x=1 - at.x))
            )
        return made

    def core(self, k):
        at = self.at
        spot = self.full.at[self.rows(at.shard(k, at.c), 2), :]
        src = self.mine(2, at.group) if k == 0 else spot
        return remote(src, spot, self.sends.at[21 + k], self.cores.at[k], at.device(c=1 - at.c))

    def local(self):
        at = self.at
        spot = self.full.at[self.rows(at.shard(0, at.c), 2), :]
        return pltpu.make_async_copy(self.mine(2, at.group), spot, self.sem_local)

    def begin(self):
        for copy in self.copies(0, 0):
            copy.start()

        @pl.when(self.at.lead)
        def _():
            for copy in self.copies(0, 1):
                copy.start()

        self.core(0).start()
        self.local().start()

    def arrived(self, k, part):
        at = self.at
        spot = self.full.at[self.rows(at.shard(k, at.c), part), :]
        return remote(spot, spot, self.sends.at[0], self.recvs.at[k, part], at.device(c=1 - at.c))

    def first(self, k):
        self.arrived(k, 0).wait_recv()
        for copy in self.copies(k, 0):
            copy.start()

    def rest(self, k):
        self.lead(k)
        self.follow(k)

    def landed(self, k):
        if k != 4:
            self.arrived(k, 0).wait_recv()
        self.arrived(k, 1).wait_recv()

    def lead(self, k):
        @pl.when(self.at.lead)
        def _():
            self.landed(k)
            for copy in self.copies(k, 1):
                copy.start()
            self.core(k).start()

    def follow(self, k):
        @pl.when(jnp.logical_not(self.at.lead))
        def _():
            self.landed(k)
            self.core(k).start()

    def from_core(self, k):
        at = self.at
        spot = self.full.at[self.rows(at.shard(k, 1 - at.c), 2), :]
        remote(spot, spot, self.sends.at[0], self.cores.at[k], at.device(c=1 - at.c)).wait_recv()

    def near(self):
        self.local().wait()
        for k in range(4):
            self.from_core(k)

    def far(self):
        for k in range(4, 8):
            self.from_core(k)

    def sent(self):
        for k in range(8):
            for copy in self.copies(k, 0):
                copy.wait_send()
            self.core(k).wait_send()

        @pl.when(self.at.lead)
        def _():
            for k in range(8):
                for copy in self.copies(k, 1):
                    copy.wait_send()


class Scatter:
    def __init__(self, at, part, ebuf, fbuf, total, result, cross, sems):
        self.at, self.part, self.ebuf, self.fbuf, self.total, self.result = at, part, ebuf, fbuf, total, result
        self.cross = cross
        self.core_send, self.core_recv, self.far_send, self.far_recv, self.end_send, self.end_recv = sems
        self.size = ebuf.shape[1]
        self.flip = 1 - at.group
        self.half = self.size // 2

    def pair(self, n):
        return n + self.flip * (7 - 2 * n)

    def shard(self, j, c):
        return self.part.at[pl.ds(pl.multiple_of((2 * j + c) * self.size, 16), self.size), :]

    def core(self, j):
        at = self.at
        return remote(
            self.shard(j, 1 - at.c), self.ebuf.at[j], self.core_send.at[j], self.core_recv.at[j],
            at.device(c=1 - at.c),
        )

    def give(self, n):
        self.core(self.pair(n)).start()

    def out(self, j, h):
        at = self.at
        z, y = j // 2, j % 2
        to_z = at.group * 2 + z % 2
        kind = (z // 2 + at.group) % 2
        start = pl.multiple_of((2 * j + at.c) * self.size + h * self.half, 16)
        copy = remote(
            self.part.at[pl.ds(start, self.half), :], self.fbuf.at[kind, at.number],
            self.far_send.at[j, h], self.far_recv.at[kind, at.number],
            at.device(x=h, y=y, z=to_z),
        )
        away = (at.x + 2 * at.y + 4 * at.z) != (h + 2 * y + 4 * to_z)
        return copy, away

    def take(self, n):
        at = self.at
        j = self.pair(n)
        self.core(j).wait_recv()
        start = pl.multiple_of((2 * j + at.c) * self.size, 16)
        where = pl.ds(start, self.size)
        self.part[where, :] = (self.part[where, :].astype(f32) + self.ebuf[j].astype(f32)).astype(bf16)
        for h in range(2):
            copy, away = self.out(j, h)
            pl.when(away)(copy.start)

    def tap(self, t):
        @pl.when(t >= 1)
        def _():
            self.give(t - 1)

        @pl.when(t >= 2)
        def _():
            self.take(t - 2)

    def sum_far(self, kind):
        at = self.at
        z = at.z if kind == 0 else at.z2
        start = pl.multiple_of(((z * 2 + at.y) * 2 + at.c) * self.size + at.x * self.half, 16)
        self.total[...] = self.part[pl.ds(start, self.half), :].astype(f32)

        def add(m, carry):
            @pl.when(m != at.number)
            def _():
                spot = self.fbuf.at[kind, m]
                remote(
                    spot, spot, self.far_send.at[0, 0], self.far_recv.at[kind, m], at.device(c=1 - at.c)
                ).wait_recv()
                self.total[...] += spot[...].astype(f32)

            return carry

        lax.fori_loop(0, 8, add, 0)
        self.result[kind] = self.total[...].astype(bf16)
        if kind == 0:
            self.near_x().start()
        else:
            self.across().start()

    def near_x(self):
        at = self.at
        return remote(
            self.result.at[0], self.result.at[2], self.end_send.at[0], self.end_recv.at[0], at.device(x=1 - at.x)
        )

    def across(self):
        at = self.at
        return remote(
            self.result.at[1], self.cross, self.end_send.at[1], self.end_recv.at[1], at.device(z=at.z2)
        )

    def far_x(self):
        at = self.at
        return remote(
            self.cross, self.result.at[3], self.end_send.at[2], self.end_recv.at[2], at.device(x=1 - at.x)
        )

    def relay(self):
        self.across().wait_recv()
        self.far_x().start()

    def finish(self, dst):
        at = self.at
        self.near_x().wait_recv()
        self.far_x().wait_recv()
        for x, group, spot in (
            (at.x, at.group, self.result.at[0]),
            (1 - at.x, at.group, self.result.at[2]),
            (at.x, 1 - at.group, self.cross),
            (1 - at.x, 1 - at.group, self.result.at[3]),
        ):
            dst[aligned(x, self.half), aligned(group, CH)] = spot[...].astype(f32)
        self.near_x().wait_send()
        self.across().wait_send()
        self.far_x().wait_send()

    def sent(self):
        def one(j, carry):
            self.core(j).wait_send()
            for h in range(2):
                copy, away = self.out(j, h)
                pl.when(away)(copy.wait_send)
            return carry

        lax.fori_loop(0, 8, one, 0)


def cube_kernel(
    sz, images, cot, w4_in, w5_in, bias_in, masks, out, igrad, dw4, dw5, db, *scratch,
):
    bufs = scratch[:12]
    (w4, w5, part5, ebuf, fbuf, total, result, cross, bias, dbias, dsum,
     local_sem, gather_send, gather_recv, gather_core, core_send, core_recv, far_send, far_recv,
     end_send, end_recv, bias_send, bias_recv, db_send, db_recv, free_core, free_far) = scratch[12:]
    at = Place()
    work = Work(sz, images, cot, masks, out, igrad, bufs)
    gather = [
        Gather(at, given, full, local_sem.at[n], gather_send.at[n], gather_recv.at[n], gather_core.at[n])
        for n, (given, full) in enumerate(((w4_in, w4), (w5_in, w5)))
    ]
    sems = [
        (core_send.at[n], core_recv.at[n], far_send.at[n], far_recv.at[n], end_send.at[n], end_recv.at[n])
        for n in range(2)
    ]
    scatter5 = Scatter(at, part5, ebuf, fbuf, total, result, cross.at[0], sems[0])
    scatter4 = Scatter(at, w5, ebuf, fbuf, total, result, cross.at[1], sems[1])
    core = at.device(c=1 - at.c)

    barrier = pltpu.get_barrier_semaphore()

    def others(act):
        def one(m, carry):
            pl.when(m != at.number)(lambda: act(m))
            return carry

        lax.fori_loop(0, 8, one, 0)

    others(lambda m: pl.semaphore_signal(barrier, inc=1, device_id=at.cube(m), device_id_type=MESH))
    for device in (core, at.device(z=at.z2)):
        pl.semaphore_signal(barrier, inc=1, device_id=device, device_id_type=MESH)
    pl.semaphore_wait(barrier, 9)

    work.fetch_two(images)
    gather[0].begin()

    swap = remote(bias_in, bias.at[1], bias_send.at[0], bias_recv.at[0], core)
    swap.start()
    work.clear()
    work.prepare_pairs(0, 2)
    gather[0].first(4)
    swap.wait_recv()
    slot = 2 + 2 * at.y + at.low
    bias[slot] = bias_in[...] + bias[1]

    def bias_way(n):
        y, z = ((1 - at.y, at.z), (at.y, at.z1), (1 - at.y, at.z1))[n]
        return remote(
            bias.at[slot], bias.at[slot], bias_send.at[1 + n], bias_recv.at[1 + n], at.device(y=y, z=z)
        )

    def bias_from(n):
        y, low = ((1 - at.y, at.low), (at.y, 1 - at.low), (1 - at.y, 1 - at.low))[n]
        spot = bias.at[2 + 2 * y + low]
        return remote(spot, spot, bias_send.at[1 + n], bias_recv.at[1 + n], core)

    for n in range(3):
        bias_way(n).start()
    work.prepare_pairs(2, 4)
    gather[0].rest(1)
    gather[0].rest(2)
    gather[0].rest(3)
    work.prepare_pairs(4, 6)
    work.prepare(12, 0)
    work.fetch_end(images)
    work.fetch_two(cot)
    gather[0].rest(4)
    gather[1].begin()
    for n in range(3):
        bias_from(n).wait_recv()
    gather[0].near()

    def steps(plan):
        def service(t):
            for k, acts in plan.items():
                @pl.when(t == k)
                def _(acts=acts):
                    for act, *given in acts:
                        act(*given)

        return service

    def bias_rows(n):
        return jnp.concatenate([bias[2 + m, n : n + 1, :] for m in (0, 2, 1, 3)], 1)

    rows = sz.rows
    near_row, far_row = 2 * at.group, 2 - 2 * at.group

    def keep4(i, value):
        work.pre4[aligned(i, rows), :] = value

    def rest4(i, skip=None):
        kept = work.pre4[aligned(i, rows), :]
        return kept + work.lot(work.pbuf, w4, (1, far_row))(i)

    def keep5(i, value):
        high = value.astype(bf16)
        where = aligned(i + 1, rows)
        work.pbuf[where, 0:CH] = high
        work.pbuf[where, CH : 2 * CH] = (value - high.astype(f32)).astype(bf16)

    def rest5(i, skip=None):
        where = aligned(i + 1, rows)
        kept = work.pbuf[where, 0:CH].astype(f32) + work.pbuf[where, CH : 2 * CH].astype(f32)
        return kept + work.lot(work.qbuf, w5, (1, far_row))(i)

    w4_way, w5_way = gather
    work.each(work.lot(work.pbuf, w4, (near_row,)), keep4, steps({
        1: [(w4_way.lead, 5)],
        2: [(w4_way.lead, 6), (w4_way.follow, 5)],
        3: [(w4_way.lead, 7), (w4_way.follow, 6)],
        4: [(w4_way.follow, 7)],
        5: [(w5_way.first, 4)],
    }))
    w4_way.far()
    work.rows13(rest4, work.finish4(bias_rows(0)), steps({
        0: [(w5_way.lead, 1), (w5_way.lead, 2), (w5_way.lead, 3)],
        1: [(w5_way.follow, 1), (w5_way.follow, 2), (w5_way.follow, 3)],
        2: [(w5_way.lead, 4)],
        3: [(w5_way.follow, 4)],
        4: [(w5_way.lead, 5)],
        5: [(w5_way.lead, 6), (w5_way.follow, 5)],
        6: [(w5_way.lead, 7), (w5_way.follow, 6)],
    }))
    w5_way.near()
    work.each(work.lot(work.qbuf, w5, (near_row,)), keep5, steps({1: [(w5_way.follow, 7)]}))
    w5_way.far()

    work.put_two(out)
    dbias[...] = jnp.zeros_like(dbias)
    db4, db5 = dbias.at[0, 0:8], dbias.at[0, 8:16]
    work.rows13(rest5, work.finish5(bias_rows(1), db5))
    work.fetch_end(cot)
    for one in gather:
        one.sent()
    swap.wait_send()
    for n in range(3):
        bias_way(n).wait_send()

    work.wgrad(work.ht, work.pbuf, w5, part5, scatter5.flip, scatter5.tap)
    scatter5.take(7)
    pl.semaphore_signal(free_core, inc=1, device_id=core, device_id_type=MESH)

    work.rows13(
        work.back(work.pbuf, w5), work.finish_back5(db4),
        steps({2: [(scatter5.sum_far, 1)], 6: [(scatter5.sum_far, 0)]}),
    )
    others(lambda m: pl.semaphore_signal(free_far, inc=1, device_id=at.cube(m), device_id_type=MESH))
    scatter5.relay()
    scatter5.sent()

    db_swap = remote(dbias.at[0], dbias.at[1], db_send.at[8], db_recv.at[8], core)
    db_swap.start()

    def db_way(m):
        return remote(dsum.at[at.number], dsum.at[at.number], db_send.at[m], db_recv.at[at.number], at.cube(m))

    def db_from(m):
        return remote(dsum.at[m], dsum.at[m], db_send.at[m], db_recv.at[m], at.cube(m))

    def tap4(t):
        @pl.when(t == 1)
        def _():
            pl.semaphore_wait(free_core, 1)

        @pl.when(t == 2)
        def _():
            scatter5.finish(dw5)
            pl.semaphore_wait(free_far, 7)

        @pl.when(t == 4)
        def _():
            db_swap.wait_recv()
            dsum[at.number] = dbias[0] + dbias[1]
            others(lambda m: db_way(m).start())

        scatter4.tap(t)

    work.wgrad(work.xt, work.qbuf, w4, w5, scatter4.flip, tap4)
    scatter4.take(7)

    work.put_end(out)
    work.put_two(igrad)
    work.rows13(
        work.back(work.qbuf, w4), work.finish_back4,
        steps({
            2: [(scatter4.sum_far, 1)],
            4: [(scatter4.relay,)],
            5: [(scatter4.sum_far, 0)],
        }),
    )
    others(lambda m: db_from(m).wait_recv())
    whole = dsum[0]
    for m in range(1, 8):
        whole = whole + dsum[m]
    db[0:1, :] = jnp.sum(whole[0:8], axis=0, keepdims=True)
    db[1:2, :] = jnp.sum(whole[8:16], axis=0, keepdims=True)
    db_swap.wait_send()
    others(lambda m: db_way(m).wait_send())
    work.put_end(igrad)
    scatter4.finish(dw4)
    scatter4.sent()


def cube_shards(images, conv4_weight, conv4_bias, conv5_weight, conv5_bias, cotangent):
    sz = Sizes(images.shape[0])
    size = conv4_weight.shape[0]
    stream = lax.axis_index("stream")
    pair = jnp.stack([conv4_bias, conv5_bias]).astype(f32)
    width = conv4_bias.shape[0]
    pair = jnp.pad(pair, ((0, 6), (0, 0)))
    blank = jnp.zeros_like(pair)
    pair = jnp.where(
        stream % 2 == 0, jnp.concatenate([pair, blank], 1), jnp.concatenate([blank, pair], 1)
    )
    vm = pl.BlockSpec(memory_space=pltpu.VMEM)
    hb = pl.BlockSpec(memory_space=pl.ANY)
    dma = pltpu.SemaphoreType.DMA
    out, igrad, dw4, dw5, db = pl.pallas_call(
        functools.partial(cube_kernel, sz),
        out_shape=(
            jax.ShapeDtypeStruct(images.shape, bf16),
            jax.ShapeDtypeStruct(images.shape, bf16),
            jax.ShapeDtypeStruct((size, 2 * CH), f32),
            jax.ShapeDtypeStruct((size, 2 * CH), f32),
            jax.ShapeDtypeStruct((2, CH), f32),
        ),
        in_specs=[hb, hb, hb, hb, vm, vm],
        out_specs=(hb, hb, vm, vm, vm),
        scratch_shapes=Work.buffers(sz)
        + [
            pltpu.VMEM((TAPS * CH, CH), bf16),
            pltpu.VMEM((TAPS * CH, CH), bf16),
            pltpu.VMEM((TAPS * CH, CH), bf16),
            pltpu.VMEM((8, size, CH), bf16),
            pltpu.VMEM((2, 8, size // 2, CH), bf16),
            pltpu.VMEM((size // 2, CH), f32),
            pltpu.VMEM((4, size // 2, CH), bf16),
            pltpu.VMEM((2, size // 2, CH), bf16),
            pltpu.VMEM((6, 8, 2 * width), f32),
            pltpu.VMEM((2, 16, CH), f32),
            pltpu.VMEM((8, 16, CH), f32),
            dma((2,)),
            dma((2, Gather.SENDS)),
            dma((2, 8, 2)),
            dma((2, 8)),
            dma((2, 8)),
            dma((2, 8)),
            dma((2, 8, 2)),
            dma((2, 2, 8)),
            dma((2, 3)),
            dma((2, 3)),
            dma((4,)),
            dma((4,)),
            dma((9,)),
            dma((9,)),
            pltpu.SemaphoreType.REGULAR,
            pltpu.SemaphoreType.REGULAR,
        ],
        compiler_params=pltpu.CompilerParams(
            vmem_limit_bytes=VMEM_LIMIT, collective_id=0, has_side_effects=True
        ),
    )(images, cotangent, conv4_weight, conv5_weight, pair, mask_rows(sz))
    own = lax.dynamic_slice_in_dim(db, stream * width % CH, width, 1)
    return out, igrad, dw4, own[0], dw5, own[1]


def solution(mesh):
    clip = P(("stream", "batch"), None, None, None)
    weight = P("stream", None)
    bias = P("stream")
    cube = dict(mesh.shape) == {"stream": 16, "batch": 2}
    return jax.shard_map(
        cube_shards if cube else plain_shards,
        mesh=mesh,
        in_specs=(clip, weight, bias, weight, bias, clip),
        out_specs=(clip, clip, weight, bias, weight, bias),
        check_vma=False,
    )
```

```python
import functools
import jax
import jax.numpy as jnp
import numpy as np
from jax import lax
from jax.experimental import pallas as pl
from jax.experimental.pallas import tpu as pltpu
from jax.sharding import PartitionSpec as P

CH = 512
SIDE = 13
TAPS = 9
ROOT = 0.7978845608
CUBE = 0.044715
VMEM_LIMIT = 64 << 20
f32 = jnp.float32
bf16 = jnp.bfloat16
MESH = pl.DeviceIdType.MESH


def tanh_part(v, v2):
    return jnp.tanh(v * (ROOT + (ROOT * CUBE) * v2))


def gelu(v):
    half = 0.5 * v
    return half + half * tanh_part(v, v * v)


def gelu_both(v):
    v2 = v * v
    t = tanh_part(v, v2)
    half = 0.5 * v
    value = half + half * t
    slope = 0.5 + 0.5 * t + half * (1.0 - t * t) * (ROOT + (3 * ROOT * CUBE) * v2)
    return value, slope


class Sizes:
    def __init__(self, clips):
        self.clips = clips
        self.used = clips * SIDE
        self.rows = -(-self.used // 16) * 16
        self.lanes = -(-self.rows // 256) * 256
        self.tall = 15 * self.rows + self.lanes - self.rows
        self.step = 8 * max(n for n in range(1, 11) if self.rows // 8 % n == 0)


def mask_rows(sz):
    row = np.arange(sz.rows)
    col = row % SIDE
    keep = row < sz.used
    table = np.stack([keep & (col != 0), keep, keep & (col != SIDE - 1)])
    return jnp.asarray(np.broadcast_to(table[:, :, None], (3, sz.rows, 128)), f32)


def aligned(index, size):
    return pl.ds(pl.multiple_of(index * size, size), size)


def flatten(sz, flat, stage):
    for n in range(sz.clips):
        flat[n * SIDE : (n + 1) * SIDE, :] = stage[n].astype(f32)


def unflatten(sz, stage, flat):
    for n in range(sz.clips):
        stage[n] = flat[n * SIDE : (n + 1) * SIDE, :].astype(bf16)


def fold8(value):
    return jnp.sum(value.reshape(value.shape[0] // 8, 8, 128), axis=0)


def columns():
    return [slice(lane, lane + 128) for lane in range(0, CH, 128)]


def nothing(step):
    return None


class Work:
    def __init__(self, sz, images, cot, masks, out, igrad, bufs):
        self.sz = sz
        self.images, self.cot, self.out, self.igrad = images, cot, out, igrad
        self.masks = masks
        (self.pbuf, self.qbuf, self.xt, self.ht, self.pre4, acc0, acc1, self.flat_in,
         self.stage_in, self.stage_out, self.in_sem, self.out_sem) = bufs
        self.accs = (acc0, acc1)

    @staticmethod
    def buffers(sz):
        rows, lanes = sz.rows, sz.lanes
        return [
            pltpu.VMEM((sz.tall, 3 * CH), bf16),
            pltpu.VMEM((sz.tall, 3 * CH), bf16),
            pltpu.VMEM((CH, SIDE * lanes), bf16),
            pltpu.VMEM((CH, SIDE * lanes), bf16),
            pltpu.VMEM((SIDE * rows, CH), f32),
            pltpu.VMEM((rows, CH), f32),
            pltpu.VMEM((rows, CH), f32),
            pltpu.VMEM((2, rows, CH), f32),
            pltpu.VMEM((2, sz.clips, SIDE, CH), bf16),
            pltpu.VMEM((2, sz.clips, SIDE, CH), bf16),
            pltpu.SemaphoreType.DMA((2,)),
            pltpu.SemaphoreType.DMA((2,)),
        ]

    def clear(self):
        sz, rows = self.sz, self.sz.rows
        for buf in (self.pbuf, self.qbuf):
            buf[0:rows, :] = jnp.zeros((rows, 3 * CH), bf16)
            buf[14 * rows : sz.tall, :] = jnp.zeros((sz.tall - 14 * rows, 3 * CH), bf16)
        self.flat_in[...] = jnp.zeros_like(self.flat_in)

    def fetch(self, src, i, slot):
        return pltpu.make_async_copy(src.at[:, i], self.stage_in.at[slot], self.in_sem.at[slot])

    def put(self, dst, i, slot):
        return pltpu.make_async_copy(self.stage_out.at[slot], dst.at[:, i], self.out_sem.at[slot])

    def fetch_two(self, src):
        self.fetch(src, 0, 0).start()
        self.fetch(src, 1, 1).start()

    def fetch_end(self, src):
        self.fetch(src, 12, 1).wait()
        self.fetch(src, 12, 0).wait()

    def put_two(self, dst):
        self.put(dst, 0, 0).start()
        self.put(dst, 1, 1).start()

    def put_end(self, dst):
        self.put(dst, 12, 1).wait()
        self.put(dst, 12, 0).wait()

    def spread(self, dst, block, cols, x, flip=False):
        low, high = (2 * CH, 0) if flip else (0, 2 * CH)
        where, lane = aligned(block, self.sz.rows), cols.start
        left = pltpu.roll(x, 1, 0) * self.masks[0]
        right = pltpu.roll(x, self.sz.rows - 1, 0) * self.masks[2]
        dst[where, low + lane : low + lane + 128] = left.astype(bf16)
        dst[where, CH + lane : CH + lane + 128] = (x * self.masks[1]).astype(bf16)
        dst[where, high + lane : high + lane + 128] = right.astype(bf16)

    def steps(self):
        return [slice(r, r + self.sz.step) for r in range(0, self.sz.rows, self.sz.step)]

    def within(self, i, some):
        start = pl.multiple_of(i * self.sz.rows, 16) + some.start
        return pl.ds(pl.multiple_of(start, 8), self.sz.step)

    def turn(self, dst, src, i):
        sz = self.sz
        value = src[aligned(i + 1, sz.rows), CH : 2 * CH]
        blank = jnp.zeros((sz.lanes - sz.rows, CH), bf16)
        dst[:, aligned(i, sz.lanes)] = jnp.concatenate([value, blank], 0).T

    def prepare(self, i, slot):
        self.fetch(self.images, i, slot).wait()
        flatten(self.sz, self.flat_in.at[slot], self.stage_in.at[slot])
        self.fetch(self.images, jnp.minimum(i + 2, 12), slot).start()
        for cols in columns():
            self.spread(self.pbuf, i + 1, cols, self.flat_in[slot, :, cols])
        self.turn(self.xt, self.pbuf, i)

    def prepare_pairs(self, first, last):
        def pair(t, carry):
            self.prepare(2 * t, 0)
            self.prepare(2 * t + 1, 1)
            return carry

        lax.fori_loop(first, last, pair, 0)

    def rows13(self, product, finish, service=nothing):
        accs = self.accs
        accs[0][...] = product(0, 0)

        def pair(t, carry):
            i = 2 * t
            service(t)
            accs[1][...] = product(i + 1)
            finish(i, accs[0], 0)
            accs[0][...] = product(i + 2)
            finish(i + 1, accs[1], 1)
            return carry

        lax.fori_loop(0, 5, pair, 0)
        service(5)
        accs[1][...] = product(11)
        finish(10, accs[0], 0)
        service(6)
        accs[0][...] = product(12, 2)
        finish(11, accs[1], 1)
        finish(12, accs[0], 0)

    def conv(self, src, w):
        rows = self.sz.rows

        def product(i, skip=None):
            total = None
            for a in range(3):
                if a == skip:
                    continue
                term = jnp.dot(
                    src[aligned(i + a, rows), :],
                    w[a * 3 * CH : (a + 1) * 3 * CH, :],
                    preferred_element_type=f32,
                )
                total = term if total is None else total + term
            return total

        return product

    def lot(self, src, w, taps):
        rows = self.sz.rows

        def product(i, skip=None):
            total = None
            for a in taps:
                term = jnp.dot(
                    src[aligned(i + a, rows), :], w[aligned(a, 3 * CH), :], preferred_element_type=f32
                )
                total = term if total is None else total + term
            return total

        return product

    def each(self, product, store, service=nothing):
        def pair(t, carry):
            service(t)
            store(2 * t, product(2 * t))
            store(2 * t + 1, product(2 * t + 1))
            return carry

        lax.fori_loop(0, 6, pair, 0)
        store(12, product(12))

    def back(self, src, w):
        rows = self.sz.rows

        def product(i, skip=None):
            total = None
            for a in range(3):
                if skip is not None and a == 2 - skip:
                    continue
                term = jnp.dot(
                    src[aligned(i + 2 - a, rows), :],
                    w[a * 3 * CH : (a + 1) * 3 * CH, :],
                    preferred_element_type=f32,
                )
                total = term if total is None else total + term
            return total

        return product

    def wgrad(self, left, src, w, dst, flip=None, service=nothing):
        rows, lanes = self.sz.rows, self.sz.lanes

        def one(t, carry):
            tap = t if flip is None else t + flip * (TAPS - 1 - 2 * t)
            a, b = tap // 3, tap % 3
            total = None
            for q in range(13):
                start = pl.multiple_of((q + 2 - a) * rows, 16)
                term = jnp.dot(
                    left[:, q * lanes : (q + 1) * lanes],
                    src[pl.ds(start, lanes), aligned(b, CH)],
                    preferred_element_type=f32,
                )
                total = term if total is None else total + term
            w[aligned(tap, CH), :] = w[aligned(tap, CH), :].T
            dst[aligned(tap, CH), :] = total.astype(dst.dtype)
            service(t)
            return carry

        lax.fori_loop(0, TAPS, one, 0)

    def finish4(self, b4):
        def finish(i, acc, slot):
            for cols in columns():
                parts = []
                for some in self.steps():
                    v = acc[some, cols] + b4[:, cols]
                    self.pre4[self.within(i, some), cols] = v
                    parts.append(gelu(v))
                self.spread(self.qbuf, i + 1, cols, jnp.concatenate(parts, 0))
            self.turn(self.ht, self.qbuf, i)

        return finish

    def finish5(self, b5, db5):
        def finish(i, acc, slot):
            self.put(self.out, i, slot).wait()
            self.fetch(self.cot, i, slot).wait()
            flatten(self.sz, self.flat_in.at[slot], self.stage_in.at[slot])
            self.fetch(self.cot, jnp.minimum(i + 2, 12), slot).start()
            for cols in columns():
                parts, total = [], db5[:, cols]
                for some in self.steps():
                    value, slope = gelu_both(acc[some, cols] + b5[:, cols])
                    acc[some, cols] = value
                    g = (self.flat_in[slot, some, cols] * slope).astype(bf16).astype(f32)
                    total = total + fold8(g)
                    parts.append(g)
                db5[:, cols] = total
                self.spread(self.pbuf, i + 1, cols, jnp.concatenate(parts, 0), True)
            unflatten(self.sz, self.stage_out.at[slot], acc)
            self.put(self.out, i, slot).start()

        return finish

    def finish_back5(self, db4):
        def finish(i, acc, slot):
            for cols in columns():
                parts, total = [], db4[:, cols]
                for some in self.steps():
                    slope = gelu_both(self.pre4[self.within(i, some), cols])[1]
                    g = acc[some, cols] * slope * self.masks[1, some, :]
                    g = g.astype(bf16).astype(f32)
                    total = total + fold8(g)
                    parts.append(g)
                db4[:, cols] = total
                self.spread(self.qbuf, i + 1, cols, jnp.concatenate(parts, 0), True)

        return finish

    def finish_back4(self, i, acc, slot):
        self.put(self.igrad, i, slot).wait()
        unflatten(self.sz, self.stage_out.at[slot], acc)
        self.put(self.igrad, i, slot).start()


def alone_kernel(
    sz, images, cot, w4_in, w5_in, b4, b5, masks, out, igrad, dw4, dw5, db4, db5, *scratch,
):
    bufs, (w4, w5, sems) = scratch[:12], scratch[12:]
    loads = [
        pltpu.make_async_copy(src, dst, sems.at[n])
        for n, (src, dst) in enumerate(((w4_in, w4), (w5_in, w5)))
    ]
    for load in loads:
        load.start()
    work = Work(sz, images, cot, masks, out, igrad, bufs)
    work.clear()
    work.fetch_two(images)
    work.prepare_pairs(0, 6)
    work.prepare(12, 0)
    work.fetch_end(images)
    work.fetch_two(cot)
    for load in loads:
        load.wait()
    work.rows13(work.conv(work.pbuf, w4), work.finish4(b4[...]))
    work.put_two(out)
    db5[...] = jnp.zeros_like(db5)
    work.rows13(work.conv(work.qbuf, w5), work.finish5(b5[...], db5))
    work.fetch_end(cot)
    work.wgrad(work.ht, work.pbuf, w5, dw5)
    db4[...] = jnp.zeros_like(db4)
    work.rows13(work.back(work.pbuf, w5), work.finish_back5(db4))
    work.wgrad(work.xt, work.qbuf, w4, dw4)
    work.put_end(out)
    work.put_two(igrad)
    work.rows13(work.back(work.qbuf, w4), work.finish_back4)
    work.put_end(igrad)


def block(images, cot, w4, w5, b4, b5):
    sz = Sizes(images.shape[0])
    vm = pl.BlockSpec(memory_space=pltpu.VMEM)
    hb = pl.BlockSpec(memory_space=pl.ANY)
    return pl.pallas_call(
        functools.partial(alone_kernel, sz),
        out_shape=(
            jax.ShapeDtypeStruct(images.shape, bf16),
            jax.ShapeDtypeStruct(images.shape, bf16),
            jax.ShapeDtypeStruct((TAPS * CH, CH), bf16),
            jax.ShapeDtypeStruct((TAPS * CH, CH), bf16),
            jax.ShapeDtypeStruct((8, CH), f32),
            jax.ShapeDtypeStruct((8, CH), f32),
        ),
        in_specs=[hb, hb, hb, hb, vm, vm, vm],
        out_specs=(hb, hb, vm, vm, vm, vm),
        scratch_shapes=Work.buffers(sz)
        + [
            pltpu.VMEM((TAPS * CH, CH), bf16),
            pltpu.VMEM((TAPS * CH, CH), bf16),
            pltpu.SemaphoreType.DMA((2,)),
        ],
        compiler_params=pltpu.CompilerParams(vmem_limit_bytes=VMEM_LIMIT),
    )(images, cot, w4, w5, b4.reshape(1, CH).astype(f32), b5.reshape(1, CH).astype(f32), mask_rows(sz))


def plain_shards(images, conv4_weight, conv4_bias, conv5_weight, conv5_bias, cotangent):
    half = lax.axis_size("stream") // 2
    group = lax.axis_index("stream") // half
    weights = lax.all_gather(
        jnp.concatenate([conv4_weight, conv5_weight], 1), "stream", axis=0, tiled=True
    )
    biases = lax.all_gather(jnp.stack([conv4_bias, conv5_bias], 1), "stream", axis=0, tiled=True)
    w4 = lax.dynamic_slice_in_dim(weights, group * CH, CH, 1)
    w5 = lax.dynamic_slice_in_dim(weights, (group + 2) * CH, CH, 1)
    own = lax.dynamic_slice_in_dim(biases, group * CH, CH, 0)
    out, igrad, dw4, dw5, db4, db5 = block(images, cotangent, w4, w5, own[:, 0], own[:, 1])

    def widen(value):
        value = value.astype(f32)
        blank = jnp.zeros_like(value)
        return jnp.where(
            group == 0,
            jnp.concatenate([value, blank], -1),
            jnp.concatenate([blank, value], -1),
        )

    def reduce(value):
        value = lax.psum_scatter(widen(value), "stream", scatter_dimension=0, tiled=True)
        return lax.psum(value.astype(bf16), "batch").astype(f32)

    dw4, dw5 = reduce(dw4), reduce(dw5)
    db = lax.psum(jnp.stack([widen(db4.sum(0)), widen(db5.sum(0))]), ("stream", "batch"))
    size = conv4_bias.shape[0]
    db = lax.dynamic_slice_in_dim(db, lax.axis_index("stream") * size, size, 1)
    return out, igrad, dw4, db[0], dw5, db[1]


class Place:
    def __init__(self):
        s = lax.axis_index("stream")
        self.x = lax.axis_index("batch")
        self.c = s % 2
        self.y = (s // 2) % 2
        self.z = s // 4
        self.low = self.z % 2
        self.group = self.z // 2
        self.z1 = self.z + 1 - 2 * self.low
        self.z2 = (self.z + 2) % 4
        self.z12 = (self.z1 + 2) % 4
        self.number = self.x * 4 + self.y * 2 + self.low
        self.lead = self.c == self.x

    def device(self, x=None, y=None, z=None, c=None):
        x = self.x if x is None else x
        y = self.y if y is None else y
        z = self.z if z is None else z
        c = self.c if c is None else c
        return {"stream": (z * 2 + y) * 2 + c, "batch": x}

    def shard(self, k, c):
        z = (self.z, self.z1, self.z, self.z1, self.z2, self.z12, self.z2, self.z12)[k]
        y = self.y if k in (0, 1, 4, 5) else 1 - self.y
        return (z * 2 + y) * 2 + c

    def cube(self, m):
        return self.device(x=m // 4, y=(m // 2) % 2, z=self.group * 2 + m % 2)


def remote(src, dst, send, recv, device):
    return pltpu.make_async_remote_copy(
        src_ref=src, dst_ref=dst, send_sem=send, recv_sem=recv, device_id=device, device_id_type=MESH
    )


class Gather:
    SENDS = 29

    def __init__(self, at, given, full, sem_local, sends, recvs, cores):
        self.at, self.given, self.full = at, given, full
        self.sem_local, self.sends, self.recvs, self.cores = sem_local, sends, recvs, cores
        self.size = given.shape[0]
        self.cut = self.size * 2 // 7 // 16 * 16

    def rows(self, shard, part):
        start = (0, self.cut, 0)[part]
        size = (self.cut, self.size - self.cut, self.size)[part]
        return pl.ds(pl.multiple_of(shard * self.size + start, 16), size)

    def mine(self, part, group):
        start = (0, self.cut, 0)[part]
        size = (self.cut, self.size - self.cut, self.size)[part]
        return self.given.at[pl.ds(start, size), aligned(group, CH)]

    def ring(self, k):
        at = self.at
        ways = (at.device(y=1 - at.y, z=at.z1), at.device(z=at.z1), at.device(y=1 - at.y))
        return [
            (k + there, device, 2 + 2 * k // 4 * 3 + 2 * n)
            for n, (there, device) in enumerate(zip((3, 1, 2), ways))
        ]

    def copies(self, k, part):
        at = self.at
        spot = self.full.at[self.rows(at.shard(k, at.c), part), :]
        src = self.mine(part, at.group) if k == 0 else spot
        made = []
        if k == 0:
            made.append(
                remote(
                    self.mine(part, 1 - at.group), spot,
                    self.sends.at[part], self.recvs.at[4, part], at.device(z=at.z2),
                )
            )
        if k in (0, 4):
            made += [
                remote(src, spot, self.sends.at[slot + part], self.recvs.at[there, part], device)
                for there, device, slot in self.ring(k)
            ]
        if k > 0 and part == 1:
            made.append(
                remote(spot, spot, self.sends.at[13 + k], self.recvs.at[k, 1], at.device(x=1 - at.x))
            )
        return made

    def core(self, k):
        at = self.at
        spot = self.full.at[self.rows(at.shard(k, at.c), 2), :]
        src = self.mine(2, at.group) if k == 0 else spot
        return remote(src, spot, self.sends.at[21 + k], self.cores.at[k], at.device(c=1 - at.c))

    def local(self):
        at = self.at
        spot = self.full.at[self.rows(at.shard(0, at.c), 2), :]
        return pltpu.make_async_copy(self.mine(2, at.group), spot, self.sem_local)

    def begin(self):
        for copy in self.copies(0, 0):
            copy.start()

        @pl.when(self.at.lead)
        def _():
            for copy in self.copies(0, 1):
                copy.start()

        self.core(0).start()
        self.local().start()

    def arrived(self, k, part):
        at = self.at
        spot = self.full.at[self.rows(at.shard(k, at.c), part), :]
        return remote(spot, spot, self.sends.at[0], self.recvs.at[k, part], at.device(c=1 - at.c))

    def first(self, k):
        self.arrived(k, 0).wait_recv()
        for copy in self.copies(k, 0):
            copy.start()

    def rest(self, k):
        self.lead(k)
        self.follow(k)

    def landed(self, k):
        if k != 4:
            self.arrived(k, 0).wait_recv()
        self.arrived(k, 1).wait_recv()

    def lead(self, k):
        @pl.when(self.at.lead)
        def _():
            self.landed(k)
            for copy in self.copies(k, 1):
                copy.start()
            self.core(k).start()

    def follow(self, k):
        @pl.when(jnp.logical_not(self.at.lead))
        def _():
            self.landed(k)
            self.core(k).start()

    def from_core(self, k):
        at = self.at
        spot = self.full.at[self.rows(at.shard(k, 1 - at.c), 2), :]
        remote(spot, spot, self.sends.at[0], self.cores.at[k], at.device(c=1 - at.c)).wait_recv()

    def near(self):
        self.local().wait()
        for k in range(4):
            self.from_core(k)

    def far(self):
        for k in range(4, 8):
            self.from_core(k)

    def sent(self):
        for k in range(8):
            for copy in self.copies(k, 0):
                copy.wait_send()
            self.core(k).wait_send()

        @pl.when(self.at.lead)
        def _():
            for k in range(8):
                for copy in self.copies(k, 1):
                    copy.wait_send()


class Scatter:
    def __init__(self, at, part, ebuf, fbuf, total, result, cross, sems):
        self.at, self.part, self.ebuf, self.fbuf, self.total, self.result = at, part, ebuf, fbuf, total, result
        self.cross = cross
        self.core_send, self.core_recv, self.far_send, self.far_recv, self.end_send, self.end_recv = sems
        self.size = ebuf.shape[1]
        self.flip = 1 - at.group
        self.half = self.size // 2

    def pair(self, n):
        return n + self.flip * (7 - 2 * n)

    def shard(self, j, c):
        return self.part.at[pl.ds(pl.multiple_of((2 * j + c) * self.size, 16), self.size), :]

    def core(self, j):
        at = self.at
        return remote(
            self.shard(j, 1 - at.c), self.ebuf.at[j], self.core_send.at[j], self.core_recv.at[j],
            at.device(c=1 - at.c),
        )

    def give(self, n):
        self.core(self.pair(n)).start()

    def out(self, j, h):
        at = self.at
        z, y = j // 2, j % 2
        to_z = at.group * 2 + z % 2
        kind = (z // 2 + at.group) % 2
        start = pl.multiple_of((2 * j + at.c) * self.size + h * self.half, 16)
        copy = remote(
            self.part.at[pl.ds(start, self.half), :], self.fbuf.at[kind, at.number],
            self.far_send.at[j, h], self.far_recv.at[kind, at.number],
            at.device(x=h, y=y, z=to_z),
        )
        away = (at.x + 2 * at.y + 4 * at.z) != (h + 2 * y + 4 * to_z)
        return copy, away

    def take(self, n):
        at = self.at
        j = self.pair(n)
        self.core(j).wait_recv()
        start = pl.multiple_of((2 * j + at.c) * self.size, 16)
        where = pl.ds(start, self.size)
        self.part[where, :] = (self.part[where, :].astype(f32) + self.ebuf[j].astype(f32)).astype(bf16)
        for h in range(2):
            copy, away = self.out(j, h)
            pl.when(away)(copy.start)

    def tap(self, t):
        @pl.when(t >= 1)
        def _():
            self.give(t - 1)

        @pl.when(t >= 2)
        def _():
            self.take(t - 2)

    def sum_far(self, kind):
        at = self.at
        z = at.z if kind == 0 else at.z2
        start = pl.multiple_of(((z * 2 + at.y) * 2 + at.c) * self.size + at.x * self.half, 16)
        self.total[...] = self.part[pl.ds(start, self.half), :].astype(f32)

        def add(m, carry):
            @pl.when(m != at.number)
            def _():
                spot = self.fbuf.at[kind, m]
                remote(
                    spot, spot, self.far_send.at[0, 0], self.far_recv.at[kind, m], at.device(c=1 - at.c)
                ).wait_recv()
                self.total[...] += spot[...].astype(f32)

            return carry

        lax.fori_loop(0, 8, add, 0)
        self.result[kind] = self.total[...].astype(bf16)
        if kind == 0:
            self.near_x().start()
        else:
            self.across().start()

    def near_x(self):
        at = self.at
        return remote(
            self.result.at[0], self.result.at[2], self.end_send.at[0], self.end_recv.at[0], at.device(x=1 - at.x)
        )

    def across(self):
        at = self.at
        return remote(
            self.result.at[1], self.cross, self.end_send.at[1], self.end_recv.at[1], at.device(z=at.z2)
        )

    def far_x(self):
        at = self.at
        return remote(
            self.cross, self.result.at[3], self.end_send.at[2], self.end_recv.at[2], at.device(x=1 - at.x)
        )

    def relay(self):
        self.across().wait_recv()
        self.far_x().start()

    def finish(self, dst):
        at = self.at
        self.near_x().wait_recv()
        self.far_x().wait_recv()
        for x, group, spot in (
            (at.x, at.group, self.result.at[0]),
            (1 - at.x, at.group, self.result.at[2]),
            (at.x, 1 - at.group, self.cross),
            (1 - at.x, 1 - at.group, self.result.at[3]),
        ):
            dst[aligned(x, self.half), aligned(group, CH)] = spot[...].astype(f32)
        self.near_x().wait_send()
        self.across().wait_send()
        self.far_x().wait_send()

    def sent(self):
        def one(j, carry):
            self.core(j).wait_send()
            for h in range(2):
                copy, away = self.out(j, h)
                pl.when(away)(copy.wait_send)
            return carry

        lax.fori_loop(0, 8, one, 0)


def cube_kernel(
    sz, images, cot, w4_in, w5_in, bias_in, masks, out, igrad, dw4, dw5, db, *scratch,
):
    bufs = scratch[:12]
    (w4, w5, part5, ebuf, fbuf, total, result, cross, bias, dbias, dsum,
     local_sem, gather_send, gather_recv, gather_core, core_send, core_recv, far_send, far_recv,
     end_send, end_recv, bias_send, bias_recv, db_send, db_recv, free_core, free_far) = scratch[12:]
    at = Place()
    work = Work(sz, images, cot, masks, out, igrad, bufs)
    gather = [
        Gather(at, given, full, local_sem.at[n], gather_send.at[n], gather_recv.at[n], gather_core.at[n])
        for n, (given, full) in enumerate(((w4_in, w4), (w5_in, w5)))
    ]
    sems = [
        (core_send.at[n], core_recv.at[n], far_send.at[n], far_recv.at[n], end_send.at[n], end_recv.at[n])
        for n in range(2)
    ]
    scatter5 = Scatter(at, part5, ebuf, fbuf, total, result, cross.at[0], sems[0])
    scatter4 = Scatter(at, w5, ebuf, fbuf, total, result, cross.at[1], sems[1])
    core = at.device(c=1 - at.c)

    barrier = pltpu.get_barrier_semaphore()

    def others(act):
        def one(m, carry):
            pl.when(m != at.number)(lambda: act(m))
            return carry

        lax.fori_loop(0, 8, one, 0)

    others(lambda m: pl.semaphore_signal(barrier, inc=1, device_id=at.cube(m), device_id_type=MESH))
    for device in (core, at.device(z=at.z2)):
        pl.semaphore_signal(barrier, inc=1, device_id=device, device_id_type=MESH)
    pl.semaphore_wait(barrier, 9)

    work.fetch_two(images)
    gather[0].begin()

    swap = remote(bias_in, bias.at[1], bias_send.at[0], bias_recv.at[0], core)
    swap.start()
    work.clear()
    work.prepare_pairs(0, 2)
    gather[0].first(4)
    swap.wait_recv()
    slot = 2 + 2 * at.y + at.low
    bias[slot] = bias_in[...] + bias[1]

    def bias_way(n):
        y, z = ((1 - at.y, at.z), (at.y, at.z1), (1 - at.y, at.z1))[n]
        return remote(
            bias.at[slot], bias.at[slot], bias_send.at[1 + n], bias_recv.at[1 + n], at.device(y=y, z=z)
        )

    def bias_from(n):
        y, low = ((1 - at.y, at.low), (at.y, 1 - at.low), (1 - at.y, 1 - at.low))[n]
        spot = bias.at[2 + 2 * y + low]
        return remote(spot, spot, bias_send.at[1 + n], bias_recv.at[1 + n], core)

    for n in range(3):
        bias_way(n).start()
    work.prepare_pairs(2, 4)
    gather[0].rest(1)
    gather[0].rest(2)
    gather[0].rest(3)
    work.prepare_pairs(4, 6)
    work.prepare(12, 0)
    work.fetch_end(images)
    work.fetch_two(cot)
    gather[0].rest(4)
    gather[1].begin()
    for n in range(3):
        bias_from(n).wait_recv()
    gather[0].near()

    def steps(plan):
        def service(t):
            for k, acts in plan.items():
                @pl.when(t == k)
                def _(acts=acts):
                    for act, *given in acts:
                        act(*given)

        return service

    def bias_rows(n):
        return jnp.concatenate([bias[2 + m, n : n + 1, :] for m in (0, 2, 1, 3)], 1)

    rows = sz.rows
    near_row, far_row = 2 * at.group, 2 - 2 * at.group

    def keep4(i, value):
        work.pre4[aligned(i, rows), :] = value

    def rest4(i, skip=None):
        kept = work.pre4[aligned(i, rows), :]
        return kept + work.lot(work.pbuf, w4, (1, far_row))(i)

    def keep5(i, value):
        high = value.astype(bf16)
        where = aligned(i + 1, rows)
        work.pbuf[where, 0:CH] = high
        work.pbuf[where, CH : 2 * CH] = (value - high.astype(f32)).astype(bf16)

    def rest5(i, skip=None):
        where = aligned(i + 1, rows)
        kept = work.pbuf[where, 0:CH].astype(f32) + work.pbuf[where, CH : 2 * CH].astype(f32)
        return kept + work.lot(work.qbuf, w5, (1, far_row))(i)

    w4_way, w5_way = gather
    work.each(work.lot(work.pbuf, w4, (near_row,)), keep4, steps({
        1: [(w4_way.lead, 5)],
        2: [(w4_way.lead, 6), (w4_way.follow, 5)],
        3: [(w4_way.lead, 7), (w4_way.follow, 6)],
        4: [(w4_way.follow, 7)],
        5: [(w5_way.first, 4)],
    }))
    w4_way.far()
    work.rows13(rest4, work.finish4(bias_rows(0)), steps({
        0: [(w5_way.lead, 1), (w5_way.lead, 2), (w5_way.lead, 3)],
        1: [(w5_way.follow, 1), (w5_way.follow, 2), (w5_way.follow, 3)],
        2: [(w5_way.lead, 4)],
        3: [(w5_way.follow, 4)],
        4: [(w5_way.lead, 5)],
        5: [(w5_way.lead, 6), (w5_way.follow, 5)],
        6: [(w5_way.lead, 7), (w5_way.follow, 6)],
    }))
    w5_way.near()
    work.each(work.lot(work.qbuf, w5, (near_row,)), keep5, steps({1: [(w5_way.follow, 7)]}))
    w5_way.far()

    work.put_two(out)
    dbias[...] = jnp.zeros_like(dbias)
    db4, db5 = dbias.at[0, 0:8], dbias.at[0, 8:16]
    work.rows13(rest5, work.finish5(bias_rows(1), db5))
    work.fetch_end(cot)
    for one in gather:
        one.sent()
    swap.wait_send()
    for n in range(3):
        bias_way(n).wait_send()

    work.wgrad(work.ht, work.pbuf, w5, part5, scatter5.flip, scatter5.tap)
    scatter5.take(7)
    pl.semaphore_signal(free_core, inc=1, device_id=core, device_id_type=MESH)

    work.rows13(
        work.back(work.pbuf, w5), work.finish_back5(db4),
        steps({2: [(scatter5.sum_far, 1)], 6: [(scatter5.sum_far, 0)]}),
    )
    others(lambda m: pl.semaphore_signal(free_far, inc=1, device_id=at.cube(m), device_id_type=MESH))
    scatter5.relay()
    scatter5.sent()

    db_swap = remote(dbias.at[0], dbias.at[1], db_send.at[8], db_recv.at[8], core)
    db_swap.start()

    def db_way(m):
        return remote(dsum.at[at.number], dsum.at[at.number], db_send.at[m], db_recv.at[at.number], at.cube(m))

    def db_from(m):
        return remote(dsum.at[m], dsum.at[m], db_send.at[m], db_recv.at[m], at.cube(m))

    def tap4(t):
        @pl.when(t == 1)
        def _():
            pl.semaphore_wait(free_core, 1)

        @pl.when(t == 2)
        def _():
            scatter5.finish(dw5)
            pl.semaphore_wait(free_far, 7)

        @pl.when(t == 4)
        def _():
            db_swap.wait_recv()
            dsum[at.number] = dbias[0] + dbias[1]
            others(lambda m: db_way(m).start())

        scatter4.tap(t)

    work.wgrad(work.xt, work.qbuf, w4, w5, scatter4.flip, tap4)
    scatter4.take(7)

    work.put_end(out)
    work.put_two(igrad)
    work.rows13(
        work.back(work.qbuf, w4), work.finish_back4,
        steps({
            2: [(scatter4.sum_far, 1)],
            5: [(scatter4.sum_far, 0)],
            6: [(scatter4.relay,)],
        }),
    )
    others(lambda m: db_from(m).wait_recv())
    whole = dsum[0]
    for m in range(1, 8):
        whole = whole + dsum[m]
    db[0:1, :] = jnp.sum(whole[0:8], axis=0, keepdims=True)
    db[1:2, :] = jnp.sum(whole[8:16], axis=0, keepdims=True)
    db_swap.wait_send()
    others(lambda m: db_way(m).wait_send())
    work.put_end(igrad)
    scatter4.finish(dw4)
    scatter4.sent()


def cube_shards(images, conv4_weight, conv4_bias, conv5_weight, conv5_bias, cotangent):
    sz = Sizes(images.shape[0])
    size = conv4_weight.shape[0]
    stream = lax.axis_index("stream")
    pair = jnp.stack([conv4_bias, conv5_bias]).astype(f32)
    width = conv4_bias.shape[0]
    pair = jnp.pad(pair, ((0, 6), (0, 0)))
    blank = jnp.zeros_like(pair)
    pair = jnp.where(
        stream % 2 == 0, jnp.concatenate([pair, blank], 1), jnp.concatenate([blank, pair], 1)
    )
    vm = pl.BlockSpec(memory_space=pltpu.VMEM)
    hb = pl.BlockSpec(memory_space=pl.ANY)
    dma = pltpu.SemaphoreType.DMA
    out, igrad, dw4, dw5, db = pl.pallas_call(
        functools.partial(cube_kernel, sz),
        out_shape=(
            jax.ShapeDtypeStruct(images.shape, bf16),
            jax.ShapeDtypeStruct(images.shape, bf16),
            jax.ShapeDtypeStruct((size, 2 * CH), f32),
            jax.ShapeDtypeStruct((size, 2 * CH), f32),
            jax.ShapeDtypeStruct((2, CH), f32),
        ),
        in_specs=[hb, hb, hb, hb, vm, vm],
        out_specs=(hb, hb, vm, vm, vm),
        scratch_shapes=Work.buffers(sz)
        + [
            pltpu.VMEM((TAPS * CH, CH), bf16),
            pltpu.VMEM((TAPS * CH, CH), bf16),
            pltpu.VMEM((TAPS * CH, CH), bf16),
            pltpu.VMEM((8, size, CH), bf16),
            pltpu.VMEM((2, 8, size // 2, CH), bf16),
            pltpu.VMEM((size // 2, CH), f32),
            pltpu.VMEM((4, size // 2, CH), bf16),
            pltpu.VMEM((2, size // 2, CH), bf16),
            pltpu.VMEM((6, 8, 2 * width), f32),
            pltpu.VMEM((2, 16, CH), f32),
            pltpu.VMEM((8, 16, CH), f32),
            dma((2,)),
            dma((2, Gather.SENDS)),
            dma((2, 8, 2)),
            dma((2, 8)),
            dma((2, 8)),
            dma((2, 8)),
            dma((2, 8, 2)),
            dma((2, 2, 8)),
            dma((2, 3)),
            dma((2, 3)),
            dma((4,)),
            dma((4,)),
            dma((9,)),
            dma((9,)),
            pltpu.SemaphoreType.REGULAR,
            pltpu.SemaphoreType.REGULAR,
        ],
        compiler_params=pltpu.CompilerParams(
            vmem_limit_bytes=VMEM_LIMIT, collective_id=0, has_side_effects=True
        ),
    )(images, cotangent, conv4_weight, conv5_weight, pair, mask_rows(sz))
    own = lax.dynamic_slice_in_dim(db, stream * width % CH, width, 1)
    return out, igrad, dw4, own[0], dw5, own[1]


def solution(mesh):
    clip = P(("stream", "batch"), None, None, None)
    weight = P("stream", None)
    bias = P("stream")
    cube = dict(mesh.shape) == {"stream": 16, "batch": 2}
    return jax.shard_map(
        cube_shards if cube else plain_shards,
        mesh=mesh,
        in_specs=(clip, weight, bias, weight, bias, clip),
        out_specs=(clip, clip, weight, bias, weight, bias),
        check_vma=False,
    )
```
